32 devices in a mesh: dp: 16 (over z, x, core), seq: 2 (over y).
Axes of the slice: x: 2, y: 2, z: 4, core: 2. Of those that a mesh axis runs over, the one named last changes fastest.
Arguments:
- tokens: bfloat16 [32, 1024, 768], P('dp', 'seq'), may hold values from -6 to 6
- segment_ids: int32 [32, 1024], P('dp', 'seq'), may hold values from 0 to 31, as said below
- w_qkv: bfloat16 [768, 2304], replicated, may hold values from -0.21875 to 0.21875
- b_qv: bfloat16 [2, 768], replicated, may hold values from -3 to 3
- w_out: bfloat16 [768, 768], replicated, may hold values from -0.875 to 0.875
- b_out: bfloat16 [768], replicated, may hold values from -3 to 3
- gain_one: bfloat16 [768], replicated, may hold values from 0.099609375 to 1.8984375
- shift_one: bfloat16 [768], replicated, may hold values from -3 to 3
- w_inner: bfloat16 [768, 3072], replicated, may hold values from -0.21875 to 0.21875
- b_inner: bfloat16 [3072], replicated, may hold values from -3 to 3
- w_final: bfloat16 [3072, 768], replicated, may hold values from -0.15625 to 0.15625
- b_final: bfloat16 [768], replicated, may hold values from -3 to 3
- gain_two: bfloat16 [768], replicated, may hold values from 0.099609375 to 1.8984375
- shift_two: bfloat16 [768], replicated, may hold values from -3 to 3
- out_grad: bfloat16 [32, 1024, 768], P('dp', 'seq'), may hold values from -6 to 6
Outputs:
- output: bfloat16 [32, 1024, 768], P('dp', 'seq')
- pooled: float32 [32, 32, 768], P('dp')
- input_grad: float32 [32, 1024, 768], P('dp', 'seq')
- grad_w_qkv: float32 [768, 2304], replicated
- grad_b_qv: float32 [2, 768], replicated
- grad_w_out: float32 [768, 768], replicated
- grad_b_out: float32 [768], replicated
- grad_gain_one: float32 [768], replicated
- grad_shift_one: float32 [768], replicated
- grad_w_inner: float32 [768, 3072], replicated
- grad_b_inner: float32 [3072], replicated
- grad_w_final: float32 [3072, 768], replicated
- grad_b_final: float32 [768], replicated
- grad_gain_two: float32 [768], replicated
- grad_shift_two: float32 [768], replicated
The draws below stay inside these ranges and needn't reach their ends.
Inputs may be any that keep to these rules, and one draw needn't show every extreme that they name: `segment_ids`: along a row the ids never fall and start at 0. In each aligned block of 2 rows exactly one row is a single sentence (all ids 0); every other row holds exactly 32 sentences of varying length, numbered 0 to 31.
All inputs are finite; a program needn't handle non-finite values.
Results may differ from the reference program's by a relative error of at most 0.014.
Values may be sent and summed in bfloat16 or wider, within the bound.
No kernel may reach another device: no remote copies, remote signals or barrier semaphores. Data moves between devices by JAX's collectives and lax.ppermute only.
A program may use at most 448 MiB of HBM per device.

```python
import math
import jax
import jax.numpy as jnp
from jax import lax

D = 768
HEADS = 12
HEAD_DIM = 64
FF = 3072
LEN = 1024
NSEG = 32
SEQS = 2
ROWS = 32


def draw_segment_ids(key, part):
    key = jax.random.fold_in(key, 11)
    perm_key, pick_key = jax.random.split(key)
    row_keys = jax.random.split(perm_key, ROWS)
    orders = jax.vmap(lambda row_key: jax.random.permutation(row_key, LEN - 1))(row_keys)
    starts = orders[:, :NSEG - 1].astype(jnp.int32) + 1
    positions = jnp.arange(LEN, dtype=jnp.int32)
    boundary = jnp.sum((positions[None, :, None] == starts[:, None, :]).astype(jnp.int32), axis=2)
    labels = jnp.cumsum(boundary, axis=1).astype(jnp.int32)
    chosen = jax.random.randint(pick_key, (ROWS // SEQS,), 0, SEQS).astype(jnp.int32)
    row_index = jnp.arange(ROWS, dtype=jnp.int32)
    single = row_index % SEQS == chosen[row_index // SEQS]
    return jnp.where(single[:, None], 0, labels).astype(jnp.int32)


def steps_of(rng, dims, shards, least, high):
    def one(dim, parts):
        draws = jax.random.uniform(jax.random.fold_in(jax.random.fold_in(rng, 6), dim), (parts,), jnp.float32, least / len(shards), high / len(shards))
        return jnp.repeat(jnp.exp(draws), dims[dim] // parts).reshape((-1,) + (1,) * (len(dims) - dim - 1))

    factor_of = one(*shards[0])
    for cut in shards[1:]:
        factor_of = factor_of * one(*cut)
    return factor_of


def scatter_about(key, extent, spread, most, cuts=(), kind=jnp.bfloat16):
    values = spread * jax.random.normal(key, extent, jnp.float32)
    if cuts:
        values = values * steps_of(key, extent, cuts, -0.22, 0.18)
    return jnp.clip(values, -most, most).astype(kind)


def setup_inputs(seed: int = 0) -> dict:
    streams_of = jax.random.split(jax.random.key(seed), 16)
    tokens = scatter_about(streams_of[0], (ROWS, LEN, D), 1.0, 6.0, ((0, 16), (1, 2)))
    segment_ids = draw_segment_ids(jax.random.fold_in(streams_of[15], 71), 0)
    w_qkv = scatter_about(streams_of[2], (D, 3 * D), D ** -0.5, 0.21875)
    b_qv = scatter_about(streams_of[3], (2, D), 0.5, 3.0)
    w_out = scatter_about(streams_of[4], (D, D), (D // 16) ** -0.5, 0.875)
    b_out = scatter_about(streams_of[5], (D,), 0.5, 3.0)
    gain_one = jnp.clip(1.0 + 0.18 * jax.random.normal(streams_of[6], (D,), jnp.float32), 0.099609375, 1.8984375).astype(jnp.bfloat16)
    shift_one = scatter_about(streams_of[7], (D,), 0.5, 3.0)
    w_inner = scatter_about(streams_of[8], (D, FF), D ** -0.5, 0.21875)
    b_inner = scatter_about(streams_of[9], (FF,), 0.5, 3.0)
    w_final = scatter_about(streams_of[10], (FF, D), (FF // 2) ** -0.5, 0.15625)
    b_final = scatter_about(streams_of[11], (D,), 0.5, 3.0)
    gain_two = jnp.clip(1.0 + 0.18 * jax.random.normal(streams_of[12], (D,), jnp.float32), 0.099609375, 1.8984375).astype(jnp.bfloat16)
    shift_two = scatter_about(streams_of[13], (D,), 0.5, 3.0)
    out_grad = scatter_about(streams_of[14], (ROWS, LEN, D), 1.0, 6.0, ((0, 16), (1, 2)))
    return {"tokens": tokens, "segment_ids": segment_ids, "w_qkv": w_qkv, "b_qv": b_qv, "w_out": w_out, "b_out": b_out, "gain_one": gain_one, "shift_one": shift_one, "w_inner": w_inner, "b_inner": b_inner, "w_final": w_final, "b_final": b_final, "gain_two": gain_two, "shift_two": shift_two, "out_grad": out_grad}


epsilon = 1e-06
highest = lax.Precision.HIGHEST

@jax.custom_vjp
def low(v):
    return lax.optimization_barrier(v.astype(jnp.bfloat16)).astype(jnp.float32)

@jax.custom_vjp
def low_back(v):
    return v

def low_keep(v):
    return (low(v), None)

def low_pass(kept, grad):
    return (grad,)

def back_keep(v):
    return (v, None)

def back_low(kept, grad):
    return (low(grad),)
low.defvjp(low_keep, low_pass)
low_back.defvjp(back_keep, back_low)

def both_round(values):
    return low_back(low(values))

def layer_norm(values, gain_row, shift_row):
    centered = values - lax.optimization_barrier(jnp.mean(values, axis=-1, keepdims=True))
    variance = lax.optimization_barrier(jnp.mean(centered * centered, axis=-1, keepdims=True))
    return centered * lax.rsqrt(variance + epsilon) * gain_row + shift_row

def gelu_exact(values):
    return jax.nn.gelu(values, approximate=False)

def project(acts, matrix):
    return jnp.einsum('gtd,de->gte', acts, matrix, precision=highest)

def forward_group(params, inputs, segment_rows):
    w_qkv, b_qv, w_out, b_out, gain_one, shift_one, w_inner, b_inner, w_final, b_final, gain_two, shift_two = params
    batch_rows = inputs.shape[0]
    merged_qkv = project(inputs, w_qkv)
    queries = both_round(merged_qkv[..., :D] + b_qv[0]).reshape(batch_rows, LEN, HEADS, HEAD_DIM)
    keys_all = both_round(merged_qkv[..., D:2 * D]).reshape(batch_rows, LEN, HEADS, HEAD_DIM)
    values_all = both_round(merged_qkv[..., 2 * D:] + b_qv[1]).reshape(batch_rows, LEN, HEADS, HEAD_DIM)
    raw_scores = jnp.einsum('gqhd,gkhd->ghqk', queries, keys_all, precision=highest)
    scores = low_back(raw_scores) * HEAD_DIM ** (-0.5)
    visible = segment_rows[:, :, None] == segment_rows[:, None, :]
    scores = jnp.where(visible[:, None], scores, -1e+30)
    probability = low(jax.nn.softmax(scores, axis=-1))
    context = jnp.einsum('ghqk,gkhd->gqhd', probability, values_all, precision=highest)
    context = both_round(context.reshape(batch_rows, LEN, D))
    attended = low_back(project(context, w_out) + b_out)
    normed = layer_norm(inputs + attended, gain_one, shift_one)
    inner_pre = low_back(project(low(normed), w_inner) + b_inner)
    activated = low(gelu_exact(inner_pre))
    final_out = low_back(project(activated, w_final) + b_final)
    layer_out = layer_norm(normed + final_out, gain_two, shift_two)
    slot_ids = jnp.arange(NSEG, dtype=jnp.int32)
    member = (segment_rows[:, :, None] == slot_ids).astype(jnp.float32)
    pool_sums = jnp.einsum('gtn,gtd->gnd', member, layer_out, precision=highest)
    counts = lax.optimization_barrier(jnp.sum(member, axis=1))
    pooled = pool_sums / jnp.maximum(counts, 1.0)[:, :, None]
    return (layer_out, pooled)

def reference(tokens, segment_ids, w_qkv, b_qv, w_out, b_out, gain_one, shift_one, w_inner, b_inner, w_final, b_final, gain_two, shift_two, out_grad):
    params = tuple((weight.astype(jnp.float32) for weight in (w_qkv, b_qv, w_out, b_out, gain_one, shift_one, w_inner, b_inner, w_final, b_final, gain_two, shift_two)))
    batch_size = math.gcd(ROWS, 4)
    shaped_in = tokens.astype(jnp.float32).reshape(ROWS // batch_size, batch_size, LEN, D)
    shaped_seg = segment_ids.reshape(ROWS // batch_size, batch_size, LEN)
    step_fn = jax.checkpoint(forward_group)

    def whole_layer(weights, layer_in):
        return lax.map(lambda batch_item: step_fn(weights, batch_item[0], batch_item[1]), (layer_in, shaped_seg))
    (layer_out, pooled), pullback = jax.vjp(whole_layer, params, shaped_in)
    pooled_zero = jnp.zeros(pooled.shape, jnp.float32)
    weight_grads, input_grad = pullback((out_grad.astype(jnp.float32).reshape(shaped_in.shape), pooled_zero))
    layer_out = layer_out.reshape(ROWS, LEN, D)
    pooled = pooled.reshape(ROWS, NSEG, D)
    return (layer_out.astype(jnp.bfloat16), pooled, input_grad.reshape(ROWS, LEN, D), weight_grads[0], weight_grads[1], weight_grads[2], weight_grads[3], weight_grads[4], weight_grads[5], weight_grads[6], weight_grads[7], weight_grads[8], weight_grads[9], weight_grads[10], weight_grads[11])
```

```python
import math

import jax
import jax.numpy as jnp
from jax import lax
from jax.experimental import pallas as pl
from jax.experimental.pallas import tpu as pltpu
from jax.sharding import PartitionSpec as P

HEADS = 12
HEAD_DIM = 64
NSEG = 32
EPSILON = 1e-06
F32 = jnp.float32
BF16 = jnp.bfloat16
FAR = 1e30
PAIR = 2 * HEAD_DIM
GROUP = 2 * PAIR
QROWS = 256
KROWS = 512
TOKENS = 256
CHUNK = 512
TAIL_RATE = 0.325
TAIL = (
    0.1296561360359192,
    0.12967278063297272,
    0.1154947280883789,
    0.0935685932636261,
    0.025895563885569572,
    0.08553703874349594,
    -0.11369360983371735,
    0.03386908397078514,
)


def dot(a, b):
    return jnp.dot(a, b, preferred_element_type=F32)


def dot_nt(a, b):
    return lax.dot_general(a, b, (((1,), (1,)), ((), ())), preferred_element_type=F32)


def dot_tn(a, b):
    return lax.dot_general(a, b, (((0,), (0,)), ((), ())), preferred_element_type=F32)


def lanes(rows):
    return lax.broadcasted_iota(jnp.int32, (rows, PAIR), 1)


def whole(shape):
    zeros = (0,) * len(shape)
    return pl.BlockSpec(shape, lambda i: zeros, pipeline_mode=pl.Buffered(1))


def pad_rows(table, devices):
    return jnp.pad(table, ((0, devices.padded(table.shape[0]) - table.shape[0]), (0, 0)))


def rows_of(count, width):
    return pl.BlockSpec((count, width), lambda i: (i, 0))


def columns_of(count, width, offset=0):
    return pl.BlockSpec((count, width), lambda i: (0, i + offset))


def params(mib):
    return pltpu.CompilerParams(
        dimension_semantics=("arbitrary",), vmem_limit_bytes=mib * 2**20
    )


def cost(flops, nbytes, exps=0):
    return pl.CostEstimate(flops=flops, bytes_accessed=nbytes, transcendentals=exps)


def split_three(values):
    high = values.astype(BF16).astype(F32)
    rest = values - high
    middle = rest.astype(BF16).astype(F32)
    return high, middle, rest - middle


def in_lanes(lane, parts, other):
    high, middle, last = parts
    return jnp.where(
        lane == NSEG,
        high,
        jnp.where(lane == NSEG + 1, middle, jnp.where(lane == NSEG + 2, last, other)),
    )


def forward_attention_kernel(
    x_ref, kext_ref, qext_ref, wq_ref, wk_ref, wv_ref, bq_ref, bv_ref,
    q_ref, k_ref, v_ref, ctx_ref, lse_ref, xt_ref,
    qx, kx, vx,
):
    group = pl.program_id(0)
    length = x_ref.shape[0]
    xt_ref[...] = x_ref[:, pl.ds(pl.multiple_of(group * GROUP, GROUP), GROUP)].astype(F32).T.astype(BF16)
    x = x_ref[...]
    queries = (dot(x, wq_ref[...]) + bq_ref[...]).astype(BF16).astype(F32) * HEAD_DIM**-0.5
    keys = dot(x, wk_ref[...]).astype(BF16)
    values = (dot(x, wv_ref[...]) + bv_ref[...]).astype(BF16)
    q_ref[...] = queries.astype(BF16)
    k_ref[...] = keys
    v_ref[...] = values
    values = values.astype(F32)
    lane = lanes(length)
    for pair in range(2):
        part = slice(pair * PAIR, (pair + 1) * PAIR)
        kx[pair, :, :PAIR] = keys[:, part]
        kx[pair, :, PAIR:] = kext_ref[...]
        for half in range(2):
            mine = (lane // HEAD_DIM) == half
            qx[2 * pair + half, :, :PAIR] = jnp.where(mine, queries[:, part], 0.0).astype(BF16)
            qx[2 * pair + half, :, PAIR:] = qext_ref[...]
            vx[2 * pair + half] = jnp.where(mine, values[:, part], 1.0).astype(BF16)

    @pl.when(group == 0)
    def _():
        lse_ref[...] = jnp.zeros_like(lse_ref)

    lane = lanes(QROWS)

    def block(i, carry):
        rows = pl.ds(pl.multiple_of(i * QROWS, QROWS), QROWS)
        lse_all = lse_ref[rows, :]

        def scores_of(head):
            return dot_nt(qx[head, rows, :], kx[head // 2])

        ahead = scores_of(0)
        for pair in range(2):
            contexts = []
            for half in range(2):
                scores = ahead
                if 2 * pair + half < 3:
                    ahead = scores_of(2 * pair + half + 1)
                row_max = jnp.max(scores, axis=1, keepdims=True)
                weights = jnp.exp(scores - row_max).astype(BF16)
                sums = dot(weights, vx[2 * pair + half])
                at = (1 - half) * HEAD_DIM
                row_total = sums[:, at : at + 1]
                contexts.append(sums / row_total)
                lse_all = jnp.where(
                    lane == group * 4 + 2 * pair + half, row_max + jnp.log(row_total), lse_all
                )
            ctx_ref[rows, pair * PAIR : (pair + 1) * PAIR] = jnp.where(
                lane < HEAD_DIM, contexts[0], contexts[1]
            ).astype(BF16)
        lse_ref[rows, :] = lse_all
        return carry

    lax.fori_loop(0, length // QROWS, block, 0)


def forward_attention(x, kext, qext, w_qkv, bias_q, bias_v):
    length, width = x.shape
    groups = width // GROUP
    wide = jax.ShapeDtypeStruct((length, width), BF16)
    return pl.pallas_call(
        forward_attention_kernel,
        grid=(groups,),
        in_specs=[
            whole((length, width)),
            whole((length, PAIR)),
            whole((length, PAIR)),
            columns_of(width, GROUP),
            columns_of(width, GROUP, groups),
            columns_of(width, GROUP, 2 * groups),
            columns_of(1, GROUP),
            columns_of(1, GROUP),
        ],
        out_specs=[columns_of(length, GROUP)] * 4
        + [whole((length, PAIR)), rows_of(GROUP, length)],
        out_shape=[wide] * 4
        + [
            jax.ShapeDtypeStruct((length, PAIR), F32),
            jax.ShapeDtypeStruct((width, length), BF16),
        ],
        scratch_shapes=[
            pltpu.VMEM((4, length, 2 * PAIR), BF16),
            pltpu.VMEM((2, length, 2 * PAIR), BF16),
            pltpu.VMEM((4, length, PAIR), BF16),
        ],
        compiler_params=params(48),
        cost_estimate=cost(24 * 10**9, 16 * 10**6, HEADS * length * length),
        name="attention_forward",
    )(x, kext, qext, w_qkv, w_qkv, w_qkv, bias_q, bias_v)


def backward_attention_kernel(last, deps, scalars, *refs):
    (
        xt_ref, kext_ref, qext_ref, lse_ref, q_ref, k_ref, v_ref, go_ref, ctx_ref,
    ) = refs[:9]
    refs = refs[9 + deps :]
    if last:
        gb_refs, refs = refs[:2], refs[2:]
        send_ref, keep_ref, merged, token, *refs = refs
    else:
        dw_ref, merged, gb_ref, token, *refs = refs
    qx, gx, kx, vx, kt, dk_acc, dv_acc = refs
    group, bit = scalars[0], scalars[1]
    token[0] = 0
    length = q_ref.shape[0]
    width = xt_ref.shape[0]
    lane = lanes(length)
    for pair in range(2):
        part = slice(pair * PAIR, (pair + 1) * PAIR)
        keys = k_ref[:, part]
        kx[:, :PAIR] = keys
        kx[:, PAIR:] = kext_ref[...]
        vx[:, :PAIR] = v_ref[:, part]
        vx[:, PAIR:] = kext_ref[...]
        kt[...] = keys.astype(F32).T.astype(BF16)
        queries = q_ref[:, part].astype(F32)
        grads = go_ref[:, part].astype(F32)
        products = grads * ctx_ref[:, part].astype(F32)
        for half in range(2):
            mine = (lane // HEAD_DIM) == half
            head = group * 4 + 2 * pair + half
            lse = jnp.sum(jnp.where(lane == head, lse_ref[...], 0.0), axis=1, keepdims=True)
            delta = jnp.sum(jnp.where(mine, products, 0.0), axis=1, keepdims=True)
            qx[half, :, :PAIR] = jnp.where(mine, queries, 0.0).astype(BF16)
            qx[half, :, PAIR:] = in_lanes(
                lane, split_three(-lse), qext_ref[...].astype(F32)
            ).astype(BF16)
            gx[half, :, :PAIR] = jnp.where(mine, grads, 0.0).astype(BF16)
            gx[half, :, PAIR:] = in_lanes(lane, split_three(-delta), 0.0).astype(BF16)
        dk_acc[...] = jnp.zeros_like(dk_acc)
        dv_acc[...] = jnp.zeros_like(dv_acc)

        def block(i, carry):
            rows = pl.ds(pl.multiple_of(i * QROWS, QROWS), QROWS)
            units = [(half, k) for k in range(0, length, KROWS) for half in range(2)]
            grad_queries = [None, None]

            def products_of(half, k):
                return (
                    dot_nt(kx[k : k + KROWS, :], qx[half, rows, :]),
                    dot_nt(vx[k : k + KROWS, :], gx[half, rows, :]),
                )

            ahead = products_of(*units[0])
            for n, (half, k) in enumerate(units):
                scores, grad_prob = ahead
                if n + 1 < len(units):
                    ahead = products_of(*units[n + 1])
                prob = jnp.exp(scores)
                grad_score = (prob * grad_prob).astype(BF16)
                dv_acc[k : k + KROWS, :] += dot(prob.astype(BF16), gx[half, rows, :PAIR])
                dk_acc[k : k + KROWS, :] += dot(grad_score, qx[half, rows, :PAIR])
                found = dot(kt[half * HEAD_DIM : (half + 1) * HEAD_DIM, k : k + KROWS], grad_score)
                grad_queries[half] = found if k == 0 else grad_queries[half] + found
            merged[rows, part] = (
                jnp.concatenate(grad_queries, axis=0).T * HEAD_DIM**-0.5
            ).astype(BF16)
            return carry

        lax.fori_loop(0, length // QROWS, block, 0)
        merged[:, GROUP + pair * PAIR : GROUP + (pair + 1) * PAIR] = dk_acc[...].astype(BF16)
        merged[:, 2 * GROUP + pair * PAIR : 2 * GROUP + (pair + 1) * PAIR] = dv_acc[
            ...
        ].astype(BF16)

    bias, found = [], []
    for j in range(3):
        grads = merged[:, j * GROUP : (j + 1) * GROUP]
        if j != 1:
            bias.append(jnp.sum(grads.astype(F32), axis=0, keepdims=True))
        dw = dot(xt_ref[...], grads).astype(BF16)
        if last:
            found.append(dw)
        else:
            dw_ref[j * width : (j + 1) * width, :] = dw
    bias = jnp.concatenate(bias + [jnp.zeros((6, GROUP), F32)], axis=0)
    if not last:
        if dw_ref.shape[0] > 3 * width:
            dw_ref[3 * width :, :] = jnp.zeros_like(dw_ref[3 * width :, :])
        gb_ref[...] = bias
        return
    half = send_ref.shape[0]
    first, second = gb_refs[0][...], gb_refs[1][...]
    lower = jnp.where(bit == 0, second, first)
    upper = jnp.where(bit == 0, first, second)
    found += [
        block.astype(BF16)
        for block in (jnp.concatenate([lower, upper], axis=0), jnp.concatenate([bias, jnp.zeros_like(bias)], axis=0))
    ]
    found.append(jnp.zeros((2 * half - 3 * width - 32, GROUP), BF16))

    def put(refs):
        at = 0
        for values in found:
            done = 0
            while done < values.shape[0]:
                which, row = (at + done) // half, (at + done) % half
                count = min(values.shape[0] - done, half - row)
                refs[which][row : row + count, :] = values[done : done + count, :]
                done += count
            at += values.shape[0]

    @pl.when(bit == 0)
    def _():
        put((keep_ref, send_ref))

    @pl.when(bit != 0)
    def _():
        put((send_ref, keep_ref))


def backward_attention(scalars, rows, biases, xt, kext, qext, lse, heads, deps):
    width, length = xt.shape
    last = bool(biases)
    fixed = lambda s: pl.BlockSpec(s, lambda i, c: (0,) * len(s), pipeline_mode=pl.Buffered(1))
    operands = [xt, kext, qext, lse, *heads, *deps, *biases]
    in_specs = [
        fixed((width, length)),
        fixed((length, PAIR)),
        fixed((length, PAIR)),
        fixed((length, PAIR)),
    ]
    in_specs += [pl.BlockSpec((length, GROUP), lambda i, c: (0, c[0]))] * 5
    in_specs += [pl.BlockSpec(memory_space=pl.ANY)] * len(deps)
    in_specs += [fixed((8, GROUP))] * len(biases)
    shape = jax.ShapeDtypeStruct
    if last:
        outs = [((rows // 2, GROUP), BF16)] * 2 + [((length, 3 * GROUP), BF16)]
    else:
        outs = [((rows, GROUP), BF16), ((length, 3 * GROUP), BF16), ((8, GROUP), F32)]

    def kernel(*refs):
        backward_attention_kernel(last, len(deps), *refs)

    return pl.pallas_call(
        kernel,
        grid_spec=pltpu.PrefetchScalarGridSpec(
            num_scalar_prefetch=1,
            grid=(1,),
            in_specs=in_specs,
            out_specs=[fixed(o[0]) for o in outs] + [pl.BlockSpec(memory_space=pltpu.SMEM)],
            scratch_shapes=[
                pltpu.VMEM((2, length, 2 * PAIR), BF16),
                pltpu.VMEM((2, length, 2 * PAIR), BF16),
                pltpu.VMEM((length, 2 * PAIR), BF16),
                pltpu.VMEM((length, 2 * PAIR), BF16),
                pltpu.VMEM((PAIR, length), BF16),
                pltpu.VMEM((length, PAIR), F32),
                pltpu.VMEM((length, PAIR), F32),
            ],
        ),
        out_shape=[shape(*o) for o in outs] + [shape((1,), jnp.int32)],
        compiler_params=params(48),
        cost_estimate=cost(24 * 10**9, 10 * 10**6, 4 * length * length),
        name="attention_backward",
    )(scalars, *operands)


def input_grad_kernel(order, resid_ref, m0_ref, m1_ref, m2_ref, w_ref, out_ref):
    width = resid_ref.shape[1]
    total = resid_ref[...]
    for i, merged in enumerate((m0_ref, m1_ref, m2_ref)):
        group = order[i]
        columns = [
            w_ref[:, pl.ds(pl.multiple_of(j * width + group * GROUP, GROUP), GROUP)]
            for j in range(3)
        ]
        total = total + dot_nt(merged[...], jnp.concatenate(columns, axis=1))
    out_ref[...] = total


def input_grad(order, resid, merged, w_qkv):
    length, width = resid.shape
    return pl.pallas_call(
        input_grad_kernel,
        grid=(length // TOKENS,),
        in_specs=[pl.BlockSpec(memory_space=pltpu.SMEM), rows_of(TOKENS, width)]
        + [rows_of(TOKENS, 3 * GROUP)] * len(merged)
        + [whole(w_qkv.shape)],
        out_specs=rows_of(TOKENS, width),
        out_shape=jax.ShapeDtypeStruct((length, width), F32),
        compiler_params=params(48),
        cost_estimate=cost(6 * length * width * width, 16 * 10**6),
        name="input_grad",
    )(order, resid, *merged, w_qkv)


def normalize(values):
    centered = values - jnp.mean(values, axis=1, keepdims=True)
    inverse = lax.rsqrt(jnp.mean(centered * centered, axis=1, keepdims=True) + EPSILON)
    return centered * inverse, inverse


def normalize_back(grads, hat, inverse):
    return inverse * (
        grads
        - jnp.mean(grads, axis=1, keepdims=True)
        - hat * jnp.mean(grads * hat, axis=1, keepdims=True)
    )


def gelu_and_slope(values):
    size = jnp.abs(values)
    under = 1.0 + TAIL_RATE * size
    t = pl.reciprocal(under, approx=True)
    t = t * (2.0 - under * t)
    t = t * (2.0 - under * t)
    poly = TAIL[-1]
    for coefficient in TAIL[-2::-1]:
        poly = poly * t + coefficient
    bell = jnp.exp(-0.5 * values * values)
    tail = poly * t * bell
    cumulative = jnp.where(values < 0, tail, 1.0 - tail)
    gelu = values * cumulative
    return gelu, cumulative + values * bell * 0.3989422804014327


def forward_dense_kernel(
    bit_ref, ctx_ref, x_ref, og_ref, kext_ref, w_out_ref, w_inner_ref, w_final_ref,
    b_out_ref, g_one_ref, s_one_ref, b_inner_ref, b_final_ref, g_two_ref, s_two_ref,
    out_ref, pooled_ref, low_ref, hat_ref, inv_ref, grad_ref, final_ref, slope_ref, send_ref, keep_ref, gb_ref,
    act, final, sums, counts, pre,
):
    step = pl.program_id(0)
    count, width = x_ref.shape
    hidden = w_inner_ref.shape[1]
    rows = pl.ds(pl.multiple_of(step * count, count), count)

    @pl.when(step == 0)
    def _():
        sums[...] = jnp.zeros_like(sums)
        counts[...] = jnp.zeros_like(counts)
        gb_ref[...] = jnp.zeros_like(gb_ref)

    resid = x_ref[...].astype(F32) + dot(ctx_ref[...], w_out_ref[...]) + b_out_ref[...]
    hat, inverse = normalize(resid)
    hat_ref[...] = hat
    inv_ref[...] = jnp.broadcast_to(inverse, inv_ref.shape)
    normed = hat * g_one_ref[...] + s_one_ref[...]
    low = normed.astype(BF16)
    low_ref[...] = low
    total = normed + b_final_ref[...]

    def inner_of(c):
        part = slice(c * CHUNK, (c + 1) * CHUNK)
        pre[c % 2] = dot(low, w_inner_ref[:, part])

    inner_of(0)
    for c in range(hidden // CHUNK):
        if c + 1 < hidden // CHUNK:
            inner_of(c + 1)
        for r in range(0, count, 32):
            for j in range(0, CHUNK, GROUP):
                part = slice(c * CHUNK + j, c * CHUNK + j + GROUP)
                inner = pre[c % 2, r : r + 32, j : j + GROUP] + b_inner_ref[:, part]
                gelu, slope = gelu_and_slope(inner)
                slope_ref[r : r + 32, part] = slope.astype(BF16)
                act[pl.ds(pl.multiple_of(step * count + r, 32), 32), part] = gelu.astype(BF16)
        part = slice(c * CHUNK, (c + 1) * CHUNK)
        total = total + dot(act[rows, part], w_final_ref[part, :])
    hat, inverse = normalize(total)
    layer_out = hat * g_two_ref[...] + s_two_ref[...]
    high = layer_out.astype(BF16)
    out_ref[...] = high
    rest = (layer_out - high.astype(F32)).astype(BF16)
    member = kext_ref[...]
    sums[...] += dot_tn(member, high) + dot_tn(member, rest)
    counts[...] += dot_tn(member, jnp.ones((count, PAIR), BF16))
    grads = og_ref[...].astype(F32)
    gb_ref[0:1, :] += jnp.sum(grads * hat, axis=0, keepdims=True)
    gb_ref[1:2, :] += jnp.sum(grads, axis=0, keepdims=True)
    grads = normalize_back(grads * g_two_ref[...], hat, inverse)
    grad_ref[...] = grads
    grads = grads.astype(BF16)
    final_ref[...] = grads
    final[rows, :] = grads
    gb_ref[2:3, :] += jnp.sum(grads.astype(F32), axis=0, keepdims=True)

    @pl.when(step == pl.num_programs(0) - 1)
    def _():
        pooled_ref[...] = sums[:NSEG, :] / jnp.maximum(counts[:NSEG, :1], 1.0)

        half = send_ref.shape[0]
        for ref, which in ((send_ref, 1 - bit_ref[0]), (keep_ref, bit_ref[0])):

            def chunk(c, carry):
                here = pl.ds(pl.multiple_of(c * TOKENS, TOKENS), TOKENS)
                start = which * half + c * TOKENS

                @pl.when(start < hidden)
                def _():
                    part = pl.ds(pl.multiple_of(start, TOKENS), TOKENS)
                    ref[here, :] = dot_tn(act[:, part], final[...]).astype(BF16)

                @pl.when(start >= hidden)
                def _():
                    ref[here, :] = jnp.zeros_like(ref[here, :])

                return carry

            lax.fori_loop(0, half // TOKENS, chunk, 0)


def forward_dense(bit, rows, context, x, out_grad, kext, w_out, w_inner, w_final, vectors):
    length, width = x.shape
    hidden = w_inner.shape[1]
    shape = jax.ShapeDtypeStruct
    return pl.pallas_call(
        forward_dense_kernel,
        grid=(length // TOKENS,),
        in_specs=[pl.BlockSpec(memory_space=pltpu.SMEM)]
        + [rows_of(TOKENS, width)] * 3
        + [rows_of(TOKENS, PAIR), whole(w_out.shape), whole(w_inner.shape), whole(w_final.shape)]
        + [whole(v.shape) for v in vectors],
        out_specs=[
            rows_of(TOKENS, width),
            whole((NSEG, width)),
            rows_of(TOKENS, width),
            rows_of(TOKENS, width),
            rows_of(TOKENS, PAIR),
            rows_of(TOKENS, width),
            rows_of(TOKENS, width),
            rows_of(TOKENS, hidden),
            whole((rows // 2, width)),
            whole((rows // 2, width)),
            whole((8, width)),
        ],
        out_shape=[
            shape((length, width), BF16),
            shape((NSEG, width), F32),
            shape((length, width), BF16),
            shape((length, width), F32),
            shape((length, PAIR), F32),
            shape((length, width), F32),
            shape((length, width), BF16),
            shape((length, hidden), BF16),
            shape((rows // 2, width), BF16),
            shape((rows // 2, width), BF16),
            shape((8, width), F32),
        ],
        scratch_shapes=[
            pltpu.VMEM((length, hidden), BF16),
            pltpu.VMEM((length, width), BF16),
            pltpu.VMEM((PAIR, width), F32),
            pltpu.VMEM((PAIR, PAIR), F32),
            pltpu.VMEM((2, TOKENS, CHUNK), F32),
        ],
        compiler_params=params(56),
        cost_estimate=cost(45 * 10**9, 45 * 10**6, length * hidden),
        name="dense_forward",
    )(bit, context, x, out_grad, kext, w_out, w_inner, w_final, *vectors)


def backward_dense_kernel(deps, *refs):
    (
        final_ref, slope_ref, grad_ref, hat_ref, inv_ref,
        w_out_ref, w_inner_ref, w_final_ref, g_one_ref,
    ) = refs[:9]
    resid_ref, go_ref, inner_ref, attended_ref, gb_ref, gbi_ref, token = refs[9 + deps :]
    token[0] = 0
    step = pl.program_id(0)
    width = grad_ref.shape[1]
    hidden = w_inner_ref.shape[1]

    @pl.when(step == 0)
    def _():
        gb_ref[...] = jnp.zeros_like(gb_ref)
        gbi_ref[...] = jnp.zeros_like(gbi_ref)

    grads = grad_ref[...]
    for c in range(hidden // width):
        part = slice(c * width, (c + 1) * width)
        grad_act = dot_nt(final_ref[...], w_final_ref[part, :])
        grad_inner = (grad_act * slope_ref[:, part].astype(F32)).astype(BF16)
        inner_ref[:, part] = grad_inner
        gbi_ref[c : c + 1, :] += jnp.sum(grad_inner.astype(F32), axis=0, keepdims=True)
        grads = grads + dot_nt(grad_inner, w_inner_ref[:, part])
    hat = hat_ref[...]
    gb_ref[0:1, :] += jnp.sum(grads * hat, axis=0, keepdims=True)
    gb_ref[1:2, :] += jnp.sum(grads, axis=0, keepdims=True)
    grads = normalize_back(grads * g_one_ref[...], hat, inv_ref[:, :1])
    resid_ref[...] = grads
    low = grads.astype(BF16)
    gb_ref[2:3, :] += jnp.sum(low.astype(F32), axis=0, keepdims=True)
    attended_ref[...] = low
    go_ref[...] = dot_nt(low, w_out_ref[...]).astype(BF16)


def backward_dense(final, slope, grad_two, hat, inverse, w_out, w_inner, w_final, gain, deps):
    length, width = hat.shape
    hidden = w_inner.shape[1]
    shape = jax.ShapeDtypeStruct

    def kernel(*refs):
        backward_dense_kernel(len(deps), *refs)

    return pl.pallas_call(
        kernel,
        grid=(length // TOKENS,),
        in_specs=[
            rows_of(TOKENS, width),
            rows_of(TOKENS, hidden),
            rows_of(TOKENS, width),
            rows_of(TOKENS, width),
            rows_of(TOKENS, PAIR),
            whole(w_out.shape),
            whole(w_inner.shape),
            whole(w_final.shape),
            whole(gain.shape),
        ]
        + [pl.BlockSpec(memory_space=pl.ANY)] * len(deps),
        out_specs=[
            rows_of(TOKENS, width),
            rows_of(TOKENS, width),
            rows_of(TOKENS, hidden),
            rows_of(TOKENS, width),
            whole((8, width)),
            whole((8, width)),
            pl.BlockSpec(memory_space=pltpu.SMEM),
        ],
        out_shape=[
            shape((length, width), F32),
            shape((length, width), BF16),
            shape((length, hidden), BF16),
            shape((length, width), BF16),
            shape((8, width), F32),
            shape((8, width), F32),
            shape((1,), jnp.int32),
        ],
        compiler_params=params(56),
        cost_estimate=cost(24 * 10**9, 40 * 10**6),
        name="dense_backward",
    )(final, slope, grad_two, hat, inverse, w_out, w_inner, w_final, gain, *deps)


def dense_weights_kernel(deps, bit_ref, *refs):
    low_ref, inner_ref, ctx_ref, attended_ref, one_ref, bi_ref, two_ref = refs[:7]
    send_ref, keep_ref, token = refs[-3:]
    token[0] = 0
    step = pl.program_id(0)
    steps = pl.num_programs(0) // 2
    width = attended_ref.shape[1]
    per = width // TOKENS
    inner_steps = bi_ref.shape[0] // 2 * per

    def one(dw_ref, block):
        @pl.when(block < inner_steps)
        def _():
            dw_ref[...] = dot_tn(low_ref[...], inner_ref[...]).astype(BF16)

        @pl.when((block >= inner_steps) & (block < inner_steps + per))
        def _():
            dw_ref[...] = dot_tn(ctx_ref[...], attended_ref[...]).astype(BF16)

        @pl.when(block >= inner_steps + per)
        def _():
            dw_ref[...] = jnp.zeros_like(dw_ref)

        @pl.when(block == inner_steps + per)
        def _():
            blocks = [one_ref[...], bi_ref[...], two_ref[...]]
            blocks.append(jnp.zeros((8, width), F32))
            dw_ref[0:32, :] = jnp.concatenate(blocks, axis=0).astype(BF16)

    @pl.when(step < steps)
    def _():
        one(send_ref, (1 - bit_ref[0]) * steps + step)

    @pl.when(step >= steps)
    def _():
        one(keep_ref, bit_ref[0] * steps + step - steps)


def dense_weights(bit, rows, low, inner, context, attended, gb_one, gb_inner, gb_two, deps):
    length, width = low.shape
    hidden = inner.shape[1]
    per = width // TOKENS
    blocks = hidden // width
    steps = rows // TOKENS // 2

    def kernel(*refs):
        dense_weights_kernel(len(deps), *refs)

    def fixed(shape):
        return pl.BlockSpec(shape, lambda i, b: (0, 0), pipeline_mode=pl.Buffered(1))

    def at(i, b):
        return jnp.where(i < steps, (1 - b[0]) * steps + i, b[0] * steps + i - steps)

    def inner_at(i, b):
        return jnp.minimum(at(i, b), blocks * per - 1)

    half = jax.ShapeDtypeStruct((rows // 2, width), BF16)
    return pl.pallas_call(
        kernel,
        grid_spec=pltpu.PrefetchScalarGridSpec(
            num_scalar_prefetch=1,
            grid=(2 * steps,),
            in_specs=[
                pl.BlockSpec((length, TOKENS), lambda i, b: (0, inner_at(i, b) % per)),
                pl.BlockSpec((length, width), lambda i, b: (0, inner_at(i, b) // per)),
                pl.BlockSpec(
                    (length, TOKENS),
                    lambda i, b: (0, jnp.clip(at(i, b) - blocks * per, 0, per - 1)),
                ),
                fixed((length, width)),
                fixed((8, width)),
                fixed((8, width)),
                fixed((8, width)),
            ]
            + [pl.BlockSpec(memory_space=pl.ANY)] * len(deps),
            out_specs=[
                pl.BlockSpec((TOKENS, width), lambda i, b: (jnp.minimum(i, steps - 1), 0)),
                pl.BlockSpec((TOKENS, width), lambda i, b: (jnp.maximum(i - steps, 0), 0)),
                pl.BlockSpec(memory_space=pltpu.SMEM),
            ],
        ),
        out_shape=[half, half, jax.ShapeDtypeStruct((1,), jnp.int32)],
        compiler_params=params(48),
        cost_estimate=cost(18 * 10**9, 24 * 10**6),
        name="dense_weights",
    )(bit, low, inner, context, attended, gb_one, gb_inner, gb_two, *deps)


def spread(own_ref, other_ref, scalars, rows, block, put):
    half = own_ref.shape[0]
    size = math.gcd(rows, block)
    per = rows // size

    def move(ref, which):
        def one(i, carry):
            piece = (i // per) ^ scalars[2 * which]
            logical = scalars[2 * which + 1] * half + piece * rows + (i % per) * size
            here = pl.ds(pl.multiple_of(i * size, size), size)
            put(pl.multiple_of(logical, size), size, ref[here, :].astype(F32))
            return carry

        lax.fori_loop(0, half // size, one, 0)

    move(own_ref, 0)
    move(other_ref, 1)


def widen_final_kernel(rows, scalars, own_ref, other_ref, out_ref):
    def put(at, size, values):
        @pl.when(at < out_ref.shape[0])
        def _():
            out_ref[pl.ds(at, size), :] = values

    spread(own_ref, other_ref, scalars, rows, out_ref.shape[1], put)


def widen_inner_kernel(rows, scalars, own_ref, other_ref, inner_ref, out_ref, small_ref):
    width, hidden = inner_ref.shape

    def put(at, size, values):
        block = at // width
        row = pl.multiple_of(at % width, size)

        @pl.when(at < hidden)
        def _():
            inner_ref[pl.ds(row, size), pl.ds(pl.multiple_of(block * width, width), width)] = values

        @pl.when((at >= hidden) & (at < hidden + width))
        def _():
            out_ref[pl.ds(row, size), :] = values

        @pl.when((at >= hidden + width) & (at < hidden + width + small_ref.shape[0]))
        def _():
            small_ref[pl.ds(row, size), :] = values

    spread(own_ref, other_ref, scalars, rows, width, put)


def widen_early_kernel(rows, scalars, own_ref, other_ref, out_ref):
    width = out_ref.shape[0]
    table = own_ref.shape[0]

    def put(at, size, values):
        group, inside = at // table, at % table

        @pl.when(inside < 3 * width)
        def _():
            column = (inside // width) * width + group * GROUP
            row = pl.multiple_of(inside % width, size)
            out_ref[pl.ds(row, size), pl.ds(pl.multiple_of(column, GROUP), GROUP)] = values

    spread(own_ref, other_ref, scalars, rows, width, put)


def widen_late_kernel(rows, scalars, own_ref, other_ref, wide_ref, out_ref, small_ref, late, sems):
    width = late.shape[1]

    def put(at, size, values):
        row = pl.multiple_of(at % width, size)

        @pl.when(at < 3 * width)
        def _():
            late[at // width, pl.ds(row, size), :] = values

        @pl.when((at >= 3 * width) & (at < 3 * width + small_ref.shape[0]))
        def _():
            small_ref[pl.ds(row, size), :] = values

    spread(own_ref, other_ref, scalars, rows, width, put)
    copies = [
        pltpu.make_async_copy(
            late.at[j], out_ref.at[:, pl.ds((j + 1) * width - GROUP, GROUP)], sems.at[j]
        )
        for j in range(3)
    ]
    for copy in copies:
        copy.start()
    for copy in copies:
        copy.wait()


def widen_late(rows, scalars, own, other, wide):
    width = wide.shape[0]
    shape = jax.ShapeDtypeStruct
    vmem = pl.BlockSpec(memory_space=pltpu.VMEM)
    return pl.pallas_call(
        lambda *refs: widen_late_kernel(rows, *refs),
        in_specs=[pl.BlockSpec(memory_space=pltpu.SMEM), vmem, vmem, pl.BlockSpec(memory_space=pl.ANY)],
        out_specs=[pl.BlockSpec(memory_space=pl.ANY), vmem],
        out_shape=[shape(wide.shape, F32), shape((width, GROUP), F32)],
        input_output_aliases={3: 0},
        scratch_shapes=[pltpu.VMEM((3, width, GROUP), F32), pltpu.SemaphoreType.DMA((3,))],
        compiler_params=pltpu.CompilerParams(vmem_limit_bytes=32 * 2**20),
        cost_estimate=cost(0, 4 * own.size + 12 * width * GROUP),
        name="widen_late",
    )(scalars, own, other, wide)


def widen(kernel, rows, scalars, arrays, shapes, name):
    nbytes = sum(2 * a.size for a in arrays) + sum(4 * math.prod(s) for s in shapes)
    return pl.pallas_call(
        lambda *refs: kernel(rows, *refs),
        in_specs=[pl.BlockSpec(memory_space=pltpu.SMEM)]
        + [pl.BlockSpec(memory_space=pltpu.VMEM)] * len(arrays),
        out_specs=[pl.BlockSpec(memory_space=pltpu.VMEM)] * len(shapes),
        out_shape=[jax.ShapeDtypeStruct(s, F32) for s in shapes],
        compiler_params=pltpu.CompilerParams(vmem_limit_bytes=48 * 2**20),
        cost_estimate=cost(0, nbytes),
        name=name,
    )(scalars, *arrays)


def swap_rows(array, parts):
    if parts == 2:
        me = lax.axis_index("seq")
        own = lax.dynamic_index_in_dim(array, me, 0, keepdims=True)
        other = lax.dynamic_index_in_dim(array, 1 - me, 0, keepdims=True)
        got = lax.ppermute(other, "seq", [(0, 1), (1, 0)])
        return jnp.concatenate([own, got], axis=0)
    return lax.all_to_all(array, "seq", split_axis=0, concat_axis=0, tiled=True)


def swap_back(array, parts):
    if parts == 2:
        me = lax.axis_index("seq")
        got = lax.ppermute(array[1], "seq", [(0, 1), (1, 0)])
        return jnp.where(
            me == 0, jnp.stack([array[0], got]), jnp.stack([got, array[0]])
        )
    return lax.all_to_all(array, "seq", split_axis=0, concat_axis=0, tiled=True)


class Slice:
    def __init__(self, n_dp, n_seq):
        dp_bits, seq_bits = n_dp.bit_length() - 1, n_seq.bit_length() - 1
        dp = [("dp", i) for i in range(dp_bits)]
        seq = [("seq", i) for i in range(seq_bits)]
        even = dp[:1] + dp[1:2] + seq
        odd = dp[:1] + seq[:1] + dp[1:2] + seq[1:]
        self.plans = (even, odd)
        self.halvings = len(even)
        self.ways = 1 << max(dp_bits - 2, 0)
        self.bits = dp_bits + seq_bits
        self.pairs = []
        for stage in range(self.halvings):
            pairs = []
            for d in range(n_dp):
                for s in range(n_seq):
                    axis, i = self.plans[d & 1][stage]
                    to = (d ^ (1 << i), s) if axis == "dp" else (d, s ^ (1 << i))
                    pairs.append((d * n_seq + s, to[0] * n_seq + to[1]))
            self.pairs.append(pairs)
        self.far_pairs = [
            [(d, d ^ (k << 2)) for d in range(n_dp)] for k in range(self.ways)
        ]
        self.index = {"dp": lax.axis_index("dp"), "seq": lax.axis_index("seq")}
        self.core = self.index["dp"] & 1
        self.place = self.index["dp"] >> 2
        self.mine = [self.bit(stage, self.core) for stage in range(self.halvings)]

    def bit(self, stage, core):
        even, odd = [(self.index[axis] >> i) & 1 for axis, i in (p[stage] for p in self.plans)]
        return jnp.where(core == 0, even, odd)

    def swap(self, array, stage):
        return lax.ppermute(array, ("dp", "seq"), self.pairs[stage])

    def far_swap(self, array, k):
        return lax.ppermute(array, "dp", self.far_pairs[k])

    def places(self):
        result = []
        for core, half in ((self.core, self.mine[0]), (self.core ^ 1, self.mine[0] ^ 1)):
            low = 0
            for stage in range(1, self.halvings):
                low = low * 2 + self.bit(stage, core)
            result += [low * self.ways + self.place, half]
        return jnp.stack([jnp.asarray(v, jnp.int32) for v in result])

    def padded(self, rows):
        unit = max(16 << self.bits, 2 * TOKENS)
        return -(-rows // unit) * unit


def add_parts(rows, picks, keep, got):
    count, width = keep.shape[0] // rows, keep.shape[1]

    def kernel(picks_ref, keep_ref, got_ref, *out_refs):
        for i, out_ref in enumerate(out_refs):
            here = pl.ds(pl.multiple_of(picks_ref[i] * rows, rows), rows)
            out_ref[...] = (keep_ref[here, :].astype(F32) + got_ref[here, :].astype(F32)).astype(BF16)

    vmem = pl.BlockSpec(memory_space=pltpu.VMEM)
    return pl.pallas_call(
        kernel,
        in_specs=[pl.BlockSpec(memory_space=pltpu.SMEM), vmem, vmem],
        out_specs=[vmem] * count,
        out_shape=[jax.ShapeDtypeStruct((rows, width), BF16)] * count,
        compiler_params=pltpu.CompilerParams(vmem_limit_bytes=16 * 2**20),
        cost_estimate=cost(0, 6 * keep.size),
        name="add_parts",
    )(picks, keep, got)


class Table:
    def __init__(self, devices, send):
        self.devices = devices
        self.stage = 0
        self.keep = None
        self.sent = send
        self.got = devices.swap(send, 0)
        self.piece_rows = 2 * send.shape[0] >> devices.bits
        self.deps = [send]

    def advance(self, token=0):
        devices = self.devices
        last = devices.halvings
        self.stage += 1
        stage = self.stage
        if stage < last:
            bit = devices.mine[stage] + token
            keep, got = (a.reshape(2, -1, a.shape[1]) for a in (self.keep, self.got))

            def added(i):
                parts = [
                    lax.dynamic_index_in_dim(a, i, 0, keepdims=False).astype(F32)
                    for a in (keep, got)
                ]
                return (parts[0] + parts[1]).astype(BF16)

            self.sent, self.keep = added(1 - bit), added(bit)
            self.got = devices.swap(self.sent, stage)
            self.deps = [self.sent, self.keep]
        elif stage == last:
            place = devices.place + token
            picks = jnp.stack([place ^ k for k in range(devices.ways)])
            rows = self.keep.shape[0] // devices.ways
            self.keep, *self.sent = add_parts(rows, picks, self.keep, self.got)
            self.got = [devices.far_swap(a, k + 1) for k, a in enumerate(self.sent)]
            self.deps = [self.keep, *self.sent]
        elif stage == last + 1:
            total = self.keep.astype(F32)
            for a in self.got:
                total = total + a.astype(F32)
            if not isinstance(token, int):
                total = jnp.where(token == 0, total, 0.0)
            self.sent = total.astype(BF16)
            self.got = [devices.far_swap(self.sent, k) for k in range(1, devices.ways)]
            self.deps = [self.sent]
        else:
            got = self.got if isinstance(self.got, list) else [self.got]
            if not isinstance(token, int):
                got = [jnp.where(token == 0, a, self.sent) for a in got]
            self.sent = jnp.concatenate([self.sent, *got], axis=0)
            self.got = devices.swap(self.sent, 2 * last + 1 - stage)
            self.deps = [self.sent]
        return self.deps

    def finish(self):
        while self.stage < 2 * self.devices.halvings + 1:
            self.advance()
        return self.sent, self.got


def on_device(
    tokens, segment_ids, w_qkv, b_qv, w_out, b_out, gain_one, shift_one,
    w_inner, b_inner, w_final, b_final, gain_two, shift_two, out_grad,
):
    parts, local_len, width = tokens.shape
    hidden = w_inner.shape[1]
    length = parts * local_len
    x = swap_rows(tokens, parts).reshape(length, width)
    segments = swap_rows(segment_ids, parts).reshape(length, 1)
    grads_in = swap_rows(out_grad, parts).reshape(length, width)

    slot = jnp.arange(PAIR, dtype=jnp.int32)[None, :]
    same = segments == slot
    kext = jnp.where(same | ((slot >= NSEG) & (slot < NSEG + 3)), 1.0, 0.0).astype(BF16)
    qext = jnp.where(same | (slot >= NSEG), 0.0, -FAR).astype(BF16)

    def row(vector):
        return vector.astype(F32).reshape(1, -1)

    devices = Slice(lax.axis_size("dp"), lax.axis_size("seq"))
    bit = jnp.asarray(devices.mine[0], jnp.int32).reshape(1)
    q, k, v, context, lse, xt = forward_attention(
        x, kext, qext, w_qkv, row(b_qv[0]), row(b_qv[1])
    )
    vectors = [
        row(v_) for v_ in (b_out, gain_one, shift_one, b_inner, b_final, gain_two, shift_two)
    ]
    (
        output, pooled, low, hat, inverse, grad_two, grad_final, slope, send, keep, gb_two,
    ) = forward_dense(
        bit, devices.padded(hidden), context, x, grads_in, kext, w_out, w_inner, w_final, vectors
    )
    t_final = Table(devices, send)
    t_final.keep = keep
    output_block = swap_back(output.reshape(parts, local_len, width), parts)
    if parts == 2:
        me = lax.axis_index("seq")
        other = lax.ppermute(pooled, "seq", [(0, 1), (1, 0)])
        pooled_all = jnp.where(me == 0, jnp.stack([pooled, other]), jnp.stack([other, pooled]))
    else:
        pooled_all = lax.all_gather(pooled, "seq", axis=0)
    resid_grad, grad_context, grad_inner, attended, gb_one, gb_inner, token = backward_dense(
        grad_final, slope, grad_two, hat, inverse, w_out, w_inner, w_final, row(gain_one),
        t_final.deps,
    )
    send, keep, token = dense_weights(
        bit, devices.padded(hidden + width + 32), low, grad_inner, context, attended,
        gb_one, gb_inner, gb_two, t_final.advance(token[0]) + [output_block, pooled_all],
    )
    t_inner = Table(devices, send)
    t_inner.keep = keep
    heads = (q, k, v, grad_context, context)
    early_rows = devices.padded(6 * width) // 2
    late_rows = devices.padded(3 * width + 32)
    order = jnp.concatenate([1 - bit, bit, jnp.full((1,), 2, jnp.int32)])

    def attend(i, rows, biases, deps):
        scalars = jnp.concatenate([order[i : i + 1], bit])
        return backward_attention(scalars, rows, biases, xt, kext, qext, lse, heads, deps)

    deps = t_final.advance(token[0]) + t_inner.deps
    send, merged_0, gb_0, token = attend(0, early_rows, [], deps)
    t_early = Table(devices, send)
    deps = t_final.advance(token[0]) + t_inner.advance(token[0]) + t_early.deps
    t_early.keep, merged_1, gb_1, token = attend(1, early_rows, [], deps)
    deps = t_final.advance(token[0]) + t_inner.advance(token[0]) + t_early.advance(token[0])
    send, keep, merged_2, token = attend(2, late_rows, [gb_0, gb_1], deps)
    t_late = Table(devices, send)
    t_late.keep = keep
    for table in (t_final, t_inner, t_early):
        table.advance(token[0])
    grad_x = input_grad(order, resid_grad, (merged_0, merged_1, merged_2), w_qkv)
    tables = (t_late, t_early, t_inner, t_final)
    ends = [t.finish() for t in tables]
    places = devices.places()
    (wide_final,) = widen(
        widen_final_kernel, t_final.piece_rows, places, ends[3], [(hidden, width)], "widen_final"
    )
    wide_inner, wide_out, small = widen(
        widen_inner_kernel, t_inner.piece_rows, places, ends[2],
        [(width, hidden), (width, width), (width, width)], "widen_inner",
    )
    (wide_qkv,) = widen(
        widen_early_kernel, t_early.piece_rows, places, ends[1], [(width, 3 * width)], "widen_early"
    )
    wide_qkv, small_qv = widen_late(t_late.piece_rows, places, *ends[0], wide_qkv)
    grad_x = grad_x.reshape(parts, local_len, width)
    if parts == 2:
        got = lax.ppermute(grad_x[1].astype(BF16), "seq", [(0, 1), (1, 0)]).astype(F32)
        input_block = jnp.where(
            me == 0, jnp.stack([grad_x[0], got]), jnp.stack([got, grad_x[0]])
        )
    else:
        input_block = swap_back(grad_x.astype(BF16), parts).astype(F32)

    gb_qv = jnp.stack(
        [jnp.concatenate([small_qv[8 * g + j] for g in range(width // GROUP)]) for j in range(2)]
    )
    return (
        output_block,
        pooled_all,
        input_block,
        wide_qkv,
        gb_qv,
        wide_out,
        small[2],
        small[0],
        small[1],
        wide_inner,
        small[8 : 8 + hidden // width].reshape(-1),
        wide_final,
        small[18],
        small[16],
        small[17],
    )


def solution(mesh):
    rows = P("dp", "seq", None)
    return jax.shard_map(
        on_device,
        mesh=mesh,
        in_specs=(rows, P("dp", "seq")) + (P(),) * 12 + (rows,),
        out_specs=(rows, P("dp", None, None), rows) + (P(),) * 12,
        check_vma=False,
    )
```

```python
import math

import jax
import jax.numpy as jnp
from jax import lax
from jax.experimental import pallas as pl
from jax.experimental.pallas import tpu as pltpu
from jax.sharding import PartitionSpec as P

HEADS = 12
HEAD_DIM = 64
NSEG = 32
EPSILON = 1e-06
F32 = jnp.float32
BF16 = jnp.bfloat16
FAR = 1e30
PAIR = 2 * HEAD_DIM
GROUP = 2 * PAIR
QROWS = 256
KROWS = 512
TOKENS = 256
CHUNK = 768


def dot(a, b):
    return jnp.dot(a, b, preferred_element_type=F32)


def dot_nt(a, b):
    return lax.dot_general(a, b, (((1,), (1,)), ((), ())), preferred_element_type=F32)


def dot_tn(a, b):
    return lax.dot_general(a, b, (((0,), (0,)), ((), ())), preferred_element_type=F32)


def lanes(rows):
    return lax.broadcasted_iota(jnp.int32, (rows, PAIR), 1)


def whole(shape):
    zeros = (0,) * len(shape)
    return pl.BlockSpec(shape, lambda i: zeros, pipeline_mode=pl.Buffered(1))


def pad_rows(table, devices):
    return jnp.pad(table, ((0, devices.padded(table.shape[0]) - table.shape[0]), (0, 0)))


def rows_of(count, width):
    return pl.BlockSpec((count, width), lambda i: (i, 0))


def columns_of(count, width, offset=0):
    return pl.BlockSpec((count, width), lambda i: (0, i + offset))


def params(mib):
    return pltpu.CompilerParams(
        dimension_semantics=("arbitrary",), vmem_limit_bytes=mib * 2**20
    )


def cost(flops, nbytes, exps=0):
    return pl.CostEstimate(flops=flops, bytes_accessed=nbytes, transcendentals=exps)


def split_three(values):
    high = values.astype(BF16).astype(F32)
    rest = values - high
    middle = rest.astype(BF16).astype(F32)
    return high, middle, rest - middle


def in_lanes(lane, parts, other):
    high, middle, last = parts
    return jnp.where(
        lane == NSEG,
        high,
        jnp.where(lane == NSEG + 1, middle, jnp.where(lane == NSEG + 2, last, other)),
    )


def forward_attention_kernel(
    x_ref, kext_ref, qext_ref, wq_ref, wk_ref, wv_ref, bq_ref, bv_ref,
    q_ref, k_ref, v_ref, ctx_ref, lse_ref, xt_ref,
    qx, kx, vx,
):
    group = pl.program_id(0)
    length = x_ref.shape[0]
    xt_ref[...] = x_ref[:, pl.ds(pl.multiple_of(group * GROUP, GROUP), GROUP)].astype(F32).T.astype(BF16)
    x = x_ref[...]
    queries = (dot(x, wq_ref[...]) + bq_ref[...]).astype(BF16).astype(F32) * HEAD_DIM**-0.5
    keys = dot(x, wk_ref[...]).astype(BF16)
    values = (dot(x, wv_ref[...]) + bv_ref[...]).astype(BF16)
    q_ref[...] = queries.astype(BF16)
    k_ref[...] = keys
    v_ref[...] = values
    values = values.astype(F32)
    lane = lanes(length)
    for pair in range(2):
        part = slice(pair * PAIR, (pair + 1) * PAIR)
        kx[pair, :, :PAIR] = keys[:, part]
        kx[pair, :, PAIR:] = kext_ref[...]
        for half in range(2):
            mine = (lane // HEAD_DIM) == half
            qx[2 * pair + half, :, :PAIR] = jnp.where(mine, queries[:, part], 0.0).astype(BF16)
            qx[2 * pair + half, :, PAIR:] = qext_ref[...]
            vx[2 * pair + half] = jnp.where(mine, values[:, part], 1.0).astype(BF16)

    @pl.when(group == 0)
    def _():
        lse_ref[...] = jnp.zeros_like(lse_ref)

    lane = lanes(QROWS)

    def block(i, carry):
        rows = pl.ds(pl.multiple_of(i * QROWS, QROWS), QROWS)
        lse_all = lse_ref[rows, :]

        def scores_of(head):
            return dot_nt(qx[head, rows, :], kx[head // 2])

        ahead = scores_of(0)
        for pair in range(2):
            contexts = []
            for half in range(2):
                scores = ahead
                if 2 * pair + half < 3:
                    ahead = scores_of(2 * pair + half + 1)
                row_max = jnp.max(scores, axis=1, keepdims=True)
                weights = jnp.exp(scores - row_max).astype(BF16)
                sums = dot(weights, vx[2 * pair + half])
                at = (1 - half) * HEAD_DIM
                row_total = sums[:, at : at + 1]
                contexts.append(sums / row_total)
                lse_all = jnp.where(
                    lane == group * 4 + 2 * pair + half, row_max + jnp.log(row_total), lse_all
                )
            ctx_ref[rows, pair * PAIR : (pair + 1) * PAIR] = jnp.where(
                lane < HEAD_DIM, contexts[0], contexts[1]
            ).astype(BF16)
        lse_ref[rows, :] = lse_all
        return carry

    lax.fori_loop(0, length // QROWS, block, 0)


def forward_attention(x, kext, qext, w_qkv, bias_q, bias_v):
    length, width = x.shape
    groups = width // GROUP
    wide = jax.ShapeDtypeStruct((length, width), BF16)
    return pl.pallas_call(
        forward_attention_kernel,
        grid=(groups,),
        in_specs=[
            whole((length, width)),
            whole((length, PAIR)),
            whole((length, PAIR)),
            columns_of(width, GROUP),
            columns_of(width, GROUP, groups),
            columns_of(width, GROUP, 2 * groups),
            columns_of(1, GROUP),
            columns_of(1, GROUP),
        ],
        out_specs=[columns_of(length, GROUP)] * 4
        + [whole((length, PAIR)), rows_of(GROUP, length)],
        out_shape=[wide] * 4
        + [
            jax.ShapeDtypeStruct((length, PAIR), F32),
            jax.ShapeDtypeStruct((width, length), BF16),
        ],
        scratch_shapes=[
            pltpu.VMEM((4, length, 2 * PAIR), BF16),
            pltpu.VMEM((2, length, 2 * PAIR), BF16),
            pltpu.VMEM((4, length, PAIR), BF16),
        ],
        compiler_params=params(48),
        cost_estimate=cost(24 * 10**9, 16 * 10**6, HEADS * length * length),
        name="attention_forward",
    )(x, kext, qext, w_qkv, w_qkv, w_qkv, bias_q, bias_v)


def backward_attention_kernel(group, last, deps, bit_ref, *refs):
    (
        xt_ref, kext_ref, qext_ref, lse_ref, q_ref, k_ref, v_ref, go_ref, ctx_ref,
    ) = refs[:9]
    refs = refs[9 + deps :]
    if last:
        gb_refs, early_refs, refs = refs[:group], refs[group : 2 * group], refs[2 * group :]
        send_ref, keep_ref, merged, token, *refs = refs
    else:
        dw_ref, merged, gb_ref, token, *refs = refs
    qx, gx, kx, vx, kt, dk_acc, dv_acc = refs
    token[0] = 0
    length = q_ref.shape[0]
    width = xt_ref.shape[0]
    lane = lanes(length)
    for pair in range(2):
        part = slice(pair * PAIR, (pair + 1) * PAIR)
        keys = k_ref[:, part]
        kx[:, :PAIR] = keys
        kx[:, PAIR:] = kext_ref[...]
        vx[:, :PAIR] = v_ref[:, part]
        vx[:, PAIR:] = kext_ref[...]
        kt[...] = keys.astype(F32).T.astype(BF16)
        queries = q_ref[:, part].astype(F32)
        grads = go_ref[:, part].astype(F32)
        products = grads * ctx_ref[:, part].astype(F32)
        for half in range(2):
            mine = (lane // HEAD_DIM) == half
            head = group * 4 + 2 * pair + half
            lse = lse_ref[:, head : head + 1]
            delta = jnp.sum(jnp.where(mine, products, 0.0), axis=1, keepdims=True)
            qx[half, :, :PAIR] = jnp.where(mine, queries, 0.0).astype(BF16)
            qx[half, :, PAIR:] = in_lanes(
                lane, split_three(-lse), qext_ref[...].astype(F32)
            ).astype(BF16)
            gx[half, :, :PAIR] = jnp.where(mine, grads, 0.0).astype(BF16)
            gx[half, :, PAIR:] = in_lanes(lane, split_three(-delta), 0.0).astype(BF16)
        dk_acc[...] = jnp.zeros_like(dk_acc)
        dv_acc[...] = jnp.zeros_like(dv_acc)

        def block(i, carry):
            rows = pl.ds(pl.multiple_of(i * QROWS, QROWS), QROWS)
            units = [(half, k) for k in range(0, length, KROWS) for half in range(2)]
            grad_queries = [None, None]

            def products_of(half, k):
                return (
                    dot_nt(kx[k : k + KROWS, :], qx[half, rows, :]),
                    dot_nt(vx[k : k + KROWS, :], gx[half, rows, :]),
                )

            ahead = products_of(*units[0])
            for n, (half, k) in enumerate(units):
                scores, grad_prob = ahead
                if n + 1 < len(units):
                    ahead = products_of(*units[n + 1])
                prob = jnp.exp(scores)
                grad_score = (prob * grad_prob).astype(BF16)
                dv_acc[k : k + KROWS, :] += dot(prob.astype(BF16), gx[half, rows, :PAIR])
                dk_acc[k : k + KROWS, :] += dot(grad_score, qx[half, rows, :PAIR])
                found = dot(kt[half * HEAD_DIM : (half + 1) * HEAD_DIM, k : k + KROWS], grad_score)
                grad_queries[half] = found if k == 0 else grad_queries[half] + found
            merged[rows, part] = (
                jnp.concatenate(grad_queries, axis=0).T * HEAD_DIM**-0.5
            ).astype(BF16)
            return carry

        lax.fori_loop(0, length // QROWS, block, 0)
        merged[:, GROUP + pair * PAIR : GROUP + (pair + 1) * PAIR] = dk_acc[...].astype(BF16)
        merged[:, 2 * GROUP + pair * PAIR : 2 * GROUP + (pair + 1) * PAIR] = dv_acc[
            ...
        ].astype(BF16)

    bias, found = [], []
    for j in range(3):
        grads = merged[:, j * GROUP : (j + 1) * GROUP]
        if j != 1:
            bias.append(jnp.sum(grads.astype(F32), axis=0, keepdims=True))
        dw = dot(xt_ref[...], grads).astype(BF16)
        if last:
            found.append(dw)
        else:
            dw_ref[j * width : (j + 1) * width, :] = dw
    bias = jnp.concatenate(bias + [jnp.zeros((6, GROUP), F32)], axis=0)
    if not last:
        gb_ref[...] = bias
        return
    half = send_ref.shape[0]
    bias = jnp.concatenate([ref[...] for ref in gb_refs] + [bias, jnp.zeros_like(bias)], axis=0)
    found = list(early_refs) + found + [bias.astype(BF16)]
    filler = 2 * half - sum(values.shape[0] for values in found)
    if filler:
        found.append(jnp.zeros((filler, GROUP), BF16))

    def put(refs):
        at = 0
        for values in found:
            done = 0
            while done < values.shape[0]:
                which, row = (at + done) // half, (at + done) % half
                count = min(values.shape[0] - done, half - row)
                refs[which][row : row + count, :] = values[done : done + count, :]
                done += count
            at += values.shape[0]

    @pl.when(bit_ref[0] == 0)
    def _():
        put((keep_ref, send_ref))

    @pl.when(bit_ref[0] != 0)
    def _():
        put((send_ref, keep_ref))


def backward_attention(group, bit, rows, biases, early, xt, kext, qext, lse, heads, deps):
    width, length = xt.shape
    last = bool(biases)
    operands = [xt, kext, qext, lse, *heads, *deps, *biases, *early]
    in_specs = [
        whole((width, length)),
        whole((length, PAIR)),
        whole((length, PAIR)),
        whole((length, PAIR)),
    ]
    in_specs += [columns_of(length, GROUP, group)] * 5
    in_specs += [pl.BlockSpec(memory_space=pl.ANY)] * len(deps)
    in_specs += [whole((8, GROUP))] * len(biases) + [whole((3 * width, GROUP))] * len(early)
    shape = jax.ShapeDtypeStruct
    if last:
        outs = [((rows // 2, GROUP), BF16)] * 2 + [((length, 3 * GROUP), BF16)]
    else:
        outs = [((3 * width, GROUP), BF16), ((length, 3 * GROUP), BF16), ((8, GROUP), F32)]

    def kernel(*refs):
        backward_attention_kernel(group, last, len(deps), *refs)

    return pl.pallas_call(
        kernel,
        grid=(1,),
        in_specs=[pl.BlockSpec(memory_space=pltpu.SMEM)] + in_specs,
        out_specs=[whole(o[0]) for o in outs] + [pl.BlockSpec(memory_space=pltpu.SMEM)],
        scratch_shapes=[
            pltpu.VMEM((2, length, 2 * PAIR), BF16),
            pltpu.VMEM((2, length, 2 * PAIR), BF16),
            pltpu.VMEM((length, 2 * PAIR), BF16),
            pltpu.VMEM((length, 2 * PAIR), BF16),
            pltpu.VMEM((PAIR, length), BF16),
            pltpu.VMEM((length, PAIR), F32),
            pltpu.VMEM((length, PAIR), F32),
        ],
        out_shape=[shape(*o) for o in outs] + [shape((1,), jnp.int32)],
        compiler_params=params(48),
        cost_estimate=cost(8 * 10**9, 10 * 10**6, 4 * length * length),
        name="attention_backward",
    )(bit, *operands)


def input_grad_kernel(resid_ref, m0_ref, m1_ref, m2_ref, w_ref, own_ref, other_ref, token):
    token[0] = 0
    width = resid_ref.shape[1]
    total = resid_ref[...]
    for group, merged in enumerate((m0_ref, m1_ref, m2_ref)):
        columns = [
            w_ref[:, j * width + group * GROUP : j * width + (group + 1) * GROUP] for j in range(3)
        ]
        total = total + dot_nt(merged[...], jnp.concatenate(columns, axis=1))
    step = pl.program_id(0)

    @pl.when(step < pl.num_programs(0) // 2)
    def _():
        own_ref[...] = total

    @pl.when(step >= pl.num_programs(0) // 2)
    def _():
        other_ref[...] = total.astype(BF16)


def input_grad(resid, merged, w_qkv):
    length, width = resid.shape
    half = length // TOKENS // 2
    shape = jax.ShapeDtypeStruct
    return pl.pallas_call(
        input_grad_kernel,
        grid=(2 * half,),
        in_specs=[rows_of(TOKENS, width)]
        + [rows_of(TOKENS, 3 * GROUP)] * len(merged)
        + [whole(w_qkv.shape)],
        out_specs=[
            pl.BlockSpec((TOKENS, width), lambda i: (jnp.minimum(i, half - 1), 0)),
            pl.BlockSpec((TOKENS, width), lambda i: (jnp.maximum(i - half, 0), 0)),
            pl.BlockSpec(memory_space=pltpu.SMEM),
        ],
        out_shape=[
            shape((length // 2, width), F32),
            shape((length // 2, width), BF16),
            shape((1,), jnp.int32),
        ],
        compiler_params=params(48),
        cost_estimate=cost(4 * 10**9, 16 * 10**6),
        name="input_grad",
    )(resid, *merged, w_qkv)


def normalize(values):
    centered = values - jnp.mean(values, axis=1, keepdims=True)
    inverse = lax.rsqrt(jnp.mean(centered * centered, axis=1, keepdims=True) + EPSILON)
    return centered * inverse, inverse


def normalize_back(grads, hat, inverse):
    return inverse * (
        grads
        - jnp.mean(grads, axis=1, keepdims=True)
        - hat * jnp.mean(grads * hat, axis=1, keepdims=True)
    )


def gelu_and_slope(values):
    cumulative = 0.5 + 0.5 * lax.erf(values * 0.7071067811865476)
    bell = jnp.exp2(values * values * -0.7213475204444817)
    return values * cumulative, cumulative + values * bell * 0.3989422804014327


def forward_dense_kernel(
    ctx_ref, x_ref, og_ref, kext_ref, w_out_ref, w_inner_ref, w_final_ref,
    b_out_ref, g_one_ref, s_one_ref, b_inner_ref, b_final_ref, g_two_ref, s_two_ref,
    own_ref, other_ref, pooled_ref, low_ref, hat_ref, inv_ref, grad_ref, final_ref, slope_ref, dw_ref, gb_ref,
    act, final, sums, counts, pre,
):
    step = pl.program_id(0)
    count, width = x_ref.shape
    hidden = w_inner_ref.shape[1]
    rows = pl.ds(pl.multiple_of(step * count, count), count)

    @pl.when(step == 0)
    def _():
        sums[...] = jnp.zeros_like(sums)
        counts[...] = jnp.zeros_like(counts)
        gb_ref[...] = jnp.zeros_like(gb_ref)

    resid = x_ref[...].astype(F32) + dot(ctx_ref[...], w_out_ref[...]) + b_out_ref[...]
    hat, inverse = normalize(resid)
    hat_ref[...] = hat
    inv_ref[...] = jnp.broadcast_to(inverse, inv_ref.shape)
    normed = hat * g_one_ref[...] + s_one_ref[...]
    low = normed.astype(BF16)
    low_ref[...] = normed.T.astype(BF16)
    total = normed + b_final_ref[...]

    def inner_of(c):
        part = slice(c * CHUNK, (c + 1) * CHUNK)
        pre[c % 2] = dot(low, w_inner_ref[:, part])

    inner_of(0)
    for c in range(hidden // CHUNK):
        if c + 1 < hidden // CHUNK:
            inner_of(c + 1)
        for r in range(0, count, 32):
            for j in range(0, CHUNK, GROUP):
                part = slice(c * CHUNK + j, c * CHUNK + j + GROUP)
                inner = pre[c % 2, r : r + 32, j : j + GROUP] + b_inner_ref[:, part]
                gelu, slope = gelu_and_slope(inner)
                slope_ref[r : r + 32, part] = slope.astype(BF16)
                act[pl.ds(pl.multiple_of(step * count + r, 32), 32), part] = gelu.astype(BF16)
        part = slice(c * CHUNK, (c + 1) * CHUNK)
        total = total + dot(act[rows, part], w_final_ref[part, :])
    hat, inverse = normalize(total)
    layer_out = hat * g_two_ref[...] + s_two_ref[...]
    high = layer_out.astype(BF16)

    @pl.when(step < pl.num_programs(0) // 2)
    def _():
        own_ref[...] = high

    @pl.when(step >= pl.num_programs(0) // 2)
    def _():
        other_ref[...] = high

    rest = (layer_out - high.astype(F32)).astype(BF16)
    member = kext_ref[...]
    sums[...] += dot_tn(member, high) + dot_tn(member, rest)
    counts[...] += dot_tn(member, jnp.ones((count, PAIR), BF16))
    grads = og_ref[...].astype(F32)
    gb_ref[0:1, :] += jnp.sum(grads * hat, axis=0, keepdims=True)
    gb_ref[1:2, :] += jnp.sum(grads, axis=0, keepdims=True)
    grads = normalize_back(grads * g_two_ref[...], hat, inverse)
    grad_ref[...] = grads
    grads = grads.astype(BF16)
    final_ref[...] = grads
    final[:, rows] = grads.astype(F32).T.astype(BF16)
    gb_ref[2:3, :] += jnp.sum(grads.astype(F32), axis=0, keepdims=True)

    @pl.when(step == pl.num_programs(0) - 1)
    def _():
        pooled_ref[...] = sums[:NSEG, :] / jnp.maximum(counts[:NSEG, :1], 1.0)

        for c in range(hidden // width):

            def chunk(r, carry):
                here = pl.ds(pl.multiple_of(r * TOKENS, TOKENS), TOKENS)
                there = pl.ds(pl.multiple_of(c * width + r * TOKENS, TOKENS), TOKENS)
                dw_ref[there, :] = dot(
                    final[here, :], act[:, c * width : (c + 1) * width]
                ).astype(BF16)
                return carry

            lax.fori_loop(0, width // TOKENS, chunk, 0)


def forward_dense(context, x, out_grad, kext, w_out, w_inner, w_final, vectors):
    length, width = x.shape
    hidden = w_inner.shape[1]
    half = length // TOKENS // 2
    shape = jax.ShapeDtypeStruct
    return pl.pallas_call(
        forward_dense_kernel,
        grid=(length // TOKENS,),
        in_specs=[rows_of(TOKENS, width)] * 3
        + [rows_of(TOKENS, PAIR), whole(w_out.shape), whole(w_inner.shape), whole(w_final.shape)]
        + [whole(v.shape) for v in vectors],
        out_specs=[
            pl.BlockSpec((TOKENS, width), lambda i: (jnp.minimum(i, half - 1), 0)),
            pl.BlockSpec((TOKENS, width), lambda i: (jnp.maximum(i - half, 0), 0)),
            whole((NSEG, width)),
            columns_of(width, TOKENS),
            rows_of(TOKENS, width),
            rows_of(TOKENS, PAIR),
            rows_of(TOKENS, width),
            rows_of(TOKENS, width),
            rows_of(TOKENS, hidden),
            whole((hidden, width)),
            whole((8, width)),
        ],
        out_shape=[
            shape((length // 2, width), BF16),
            shape((length // 2, width), BF16),
            shape((NSEG, width), F32),
            shape((width, length), BF16),
            shape((length, width), F32),
            shape((length, PAIR), F32),
            shape((length, width), F32),
            shape((length, width), BF16),
            shape((length, hidden), BF16),
            shape((hidden, width), BF16),
            shape((8, width), F32),
        ],
        scratch_shapes=[
            pltpu.VMEM((length, hidden), BF16),
            pltpu.VMEM((width, length), BF16),
            pltpu.VMEM((PAIR, width), F32),
            pltpu.VMEM((PAIR, PAIR), F32),
            pltpu.VMEM((2, TOKENS, CHUNK), F32),
        ],
        compiler_params=params(56),
        cost_estimate=cost(45 * 10**9, 45 * 10**6, length * hidden),
        name="dense_forward",
    )(context, x, out_grad, kext, w_out, w_inner, w_final, *vectors)


def backward_dense_kernel(deps, *refs):
    (
        final_ref, slope_ref, grad_ref, hat_ref, inv_ref,
        w_out_ref, w_inner_ref, w_final_ref, g_one_ref,
    ) = refs[:9]
    resid_ref, go_ref, inner_ref, attended_ref, gb_ref, gbi_ref, token = refs[9 + deps :]
    token[0] = 0
    step = pl.program_id(0)
    width = grad_ref.shape[1]
    hidden = w_inner_ref.shape[1]

    @pl.when(step == 0)
    def _():
        gb_ref[...] = jnp.zeros_like(gb_ref)
        gbi_ref[...] = jnp.zeros_like(gbi_ref)

    grads = grad_ref[...]
    for c in range(hidden // width):
        part = slice(c * width, (c + 1) * width)
        grad_act = dot_nt(final_ref[...], w_final_ref[part, :])
        grad_inner = (grad_act * slope_ref[:, part].astype(F32)).astype(BF16)
        inner_ref[:, part] = grad_inner
        gbi_ref[c : c + 1, :] += jnp.sum(grad_inner.astype(F32), axis=0, keepdims=True)
        grads = grads + dot_nt(grad_inner, w_inner_ref[:, part])
    hat = hat_ref[...]
    gb_ref[0:1, :] += jnp.sum(grads * hat, axis=0, keepdims=True)
    gb_ref[1:2, :] += jnp.sum(grads, axis=0, keepdims=True)
    grads = normalize_back(grads * g_one_ref[...], hat, inv_ref[:, :1])
    resid_ref[...] = grads
    low = grads.astype(BF16)
    gb_ref[2:3, :] += jnp.sum(low.astype(F32), axis=0, keepdims=True)
    attended_ref[...] = low
    go_ref[...] = dot_nt(low, w_out_ref[...]).astype(BF16)


def backward_dense(final, slope, grad_two, hat, inverse, w_out, w_inner, w_final, gain, deps):
    length, width = hat.shape
    hidden = w_inner.shape[1]
    shape = jax.ShapeDtypeStruct

    def kernel(*refs):
        backward_dense_kernel(len(deps), *refs)

    return pl.pallas_call(
        kernel,
        grid=(length // TOKENS,),
        in_specs=[
            rows_of(TOKENS, width),
            rows_of(TOKENS, hidden),
            rows_of(TOKENS, width),
            rows_of(TOKENS, width),
            rows_of(TOKENS, PAIR),
            whole(w_out.shape),
            whole(w_inner.shape),
            whole(w_final.shape),
            whole(gain.shape),
        ]
        + [pl.BlockSpec(memory_space=pl.ANY)] * len(deps),
        out_specs=[
            rows_of(TOKENS, width),
            rows_of(TOKENS, width),
            rows_of(TOKENS, hidden),
            rows_of(TOKENS, width),
            whole((8, width)),
            whole((8, width)),
            pl.BlockSpec(memory_space=pltpu.SMEM),
        ],
        out_shape=[
            shape((length, width), F32),
            shape((length, width), BF16),
            shape((length, hidden), BF16),
            shape((length, width), BF16),
            shape((8, width), F32),
            shape((8, width), F32),
            shape((1,), jnp.int32),
        ],
        compiler_params=params(56),
        cost_estimate=cost(8 * 10**9, 20 * 10**6),
        name="dense_backward",
    )(final, slope, grad_two, hat, inverse, w_out, w_inner, w_final, gain, *deps)


def dense_weights_kernel(deps, bit_ref, *refs):
    low_ref, inner_ref, ctx_ref, attended_ref, one_ref, bi_ref, two_ref = refs[:7]
    send_ref, keep_ref, token = refs[-3:]
    token[0] = 0
    step = pl.program_id(0)
    steps = pl.num_programs(0) // 2
    width = attended_ref.shape[1]
    per = width // TOKENS
    inner_steps = bi_ref.shape[0] // 2 * per

    def one(dw_ref, block):
        @pl.when(block < inner_steps)
        def _():
            dw_ref[...] = dot(low_ref[...], inner_ref[...]).astype(BF16)

        @pl.when((block >= inner_steps) & (block < inner_steps + per))
        def _():
            dw_ref[...] = dot_tn(ctx_ref[...], attended_ref[...]).astype(BF16)

        @pl.when(block >= inner_steps + per)
        def _():
            dw_ref[...] = jnp.zeros_like(dw_ref)

        @pl.when(block == inner_steps + per)
        def _():
            blocks = [one_ref[...], bi_ref[...], two_ref[...]]
            blocks.append(jnp.zeros((8, width), F32))
            dw_ref[0:32, :] = jnp.concatenate(blocks, axis=0).astype(BF16)

    @pl.when(step < steps)
    def _():
        one(send_ref, (1 - bit_ref[0]) * steps + step)

    @pl.when(step >= steps)
    def _():
        one(keep_ref, bit_ref[0] * steps + step - steps)


def dense_weights(bit, rows, low, inner, context, attended, gb_one, gb_inner, gb_two, deps):
    width, length = low.shape
    hidden = inner.shape[1]
    per = width // TOKENS
    blocks = hidden // width
    steps = rows // TOKENS // 2

    def kernel(*refs):
        dense_weights_kernel(len(deps), *refs)

    def fixed(shape):
        return pl.BlockSpec(shape, lambda i, b: (0, 0), pipeline_mode=pl.Buffered(1))

    def at(i, b):
        return jnp.where(i < steps, (1 - b[0]) * steps + i, b[0] * steps + i - steps)

    def inner_at(i, b):
        return jnp.minimum(at(i, b), blocks * per - 1)

    half = jax.ShapeDtypeStruct((rows // 2, width), BF16)
    return pl.pallas_call(
        kernel,
        grid_spec=pltpu.PrefetchScalarGridSpec(
            num_scalar_prefetch=1,
            grid=(2 * steps,),
            in_specs=[
                pl.BlockSpec((TOKENS, length), lambda i, b: (inner_at(i, b) % per, 0)),
                pl.BlockSpec((length, width), lambda i, b: (0, inner_at(i, b) // per)),
                pl.BlockSpec(
                    (length, TOKENS),
                    lambda i, b: (0, jnp.clip(at(i, b) - blocks * per, 0, per - 1)),
                ),
                fixed((length, width)),
                fixed((8, width)),
                fixed((8, width)),
                fixed((8, width)),
            ]
            + [pl.BlockSpec(memory_space=pl.ANY)] * len(deps),
            out_specs=[
                pl.BlockSpec((TOKENS, width), lambda i, b: (jnp.minimum(i, steps - 1), 0)),
                pl.BlockSpec((TOKENS, width), lambda i, b: (jnp.maximum(i - steps, 0), 0)),
                pl.BlockSpec(memory_space=pltpu.SMEM),
            ],
        ),
        out_shape=[half, half, jax.ShapeDtypeStruct((1,), jnp.int32)],
        compiler_params=params(48),
        cost_estimate=cost(6 * 10**9, 16 * 10**6),
        name="dense_weights",
    )(bit, low, inner, context, attended, gb_one, gb_inner, gb_two, *deps)


def spread(own_ref, other_ref, scalars, rows, block, put):
    half = own_ref.shape[0]

    def move(ref, low, which):
        for piece in range(half // rows):
            start = which * half + piece * rows
            at = 0
            while at < rows:
                count = min(rows - at, block - (start + at) % block)
                here = pl.ds(pl.multiple_of((piece ^ low) * rows + at, math.gcd(rows, block)), count)
                put(start + at, ref[here, :].astype(F32))
                at += count

    for i, ref in enumerate((own_ref, other_ref)):
        for which in range(2):

            @pl.when(scalars[2 * i + 1] == which)
            def _():
                move(ref, scalars[2 * i], which)


def put_small(small_ref, row, values):
    count = min(values.shape[0], small_ref.shape[0] - row)
    if count > 0:
        small_ref[row : row + count, :] = values[:count, :]


def widen_inner_kernel(rows, scalars, own_ref, other_ref, inner_ref, out_ref, small_ref):
    width, hidden = inner_ref.shape

    def put(at, values):
        block, row = at // width, at % width
        here = slice(row, row + values.shape[0])
        if at < hidden:
            inner_ref[here, block * width : (block + 1) * width] = values
        elif at < hidden + width:
            out_ref[here, :] = values
        else:
            put_small(small_ref, at - hidden - width, values)

    spread(own_ref, other_ref, scalars, rows, width, put)


def widen_qkv_kernel(rows, scalars, own_ref, other_ref, out_ref, small_ref):
    width = out_ref.shape[0]

    def put(at, values):
        block, row = at // width, at % width
        if block < out_ref.shape[1] // GROUP:
            column = (block % 3) * width + (block // 3) * GROUP
            out_ref[row : row + values.shape[0], column : column + GROUP] = values
        else:
            put_small(small_ref, row + (block - out_ref.shape[1] // GROUP) * width, values)

    spread(own_ref, other_ref, scalars, rows, width, put)


def turn_kernel(low_ref, *refs):
    refs[-1][...] = low_ref[...].astype(F32).T


def turn(table, deps):
    rows, width = table.shape
    return pl.pallas_call(
        turn_kernel,
        grid=(rows // width, width // TOKENS),
        in_specs=[pl.BlockSpec((width, TOKENS), lambda b, r: (b, r))]
        + [pl.BlockSpec(memory_space=pl.ANY)] * len(deps),
        out_specs=pl.BlockSpec((TOKENS, width), lambda b, r: (b * (width // TOKENS) + r, 0)),
        out_shape=jax.ShapeDtypeStruct((rows, width), F32),
        cost_estimate=cost(0, 6 * rows * width),
        name="turn",
    )(table, *deps)


def widen(kernel, rows, scalars, arrays, shapes, name):
    nbytes = sum(2 * a.size for a in arrays) + sum(4 * math.prod(s) for s in shapes)
    return pl.pallas_call(
        lambda *refs: kernel(rows, *refs),
        in_specs=[pl.BlockSpec(memory_space=pltpu.SMEM)]
        + [pl.BlockSpec(memory_space=pltpu.VMEM)] * len(arrays),
        out_specs=[pl.BlockSpec(memory_space=pltpu.VMEM)] * len(shapes),
        out_shape=[jax.ShapeDtypeStruct(s, F32) for s in shapes],
        compiler_params=pltpu.CompilerParams(vmem_limit_bytes=48 * 2**20),
        cost_estimate=cost(0, nbytes),
        name=name,
    )(scalars, *arrays)


def swap_rows(array, parts):
    if parts == 2:
        me = lax.axis_index("seq")
        own = lax.dynamic_index_in_dim(array, me, 0, keepdims=True)
        other = lax.dynamic_index_in_dim(array, 1 - me, 0, keepdims=True)
        got = lax.ppermute(other, "seq", [(0, 1), (1, 0)])
        return jnp.concatenate([own, got], axis=0)
    return lax.all_to_all(array, "seq", split_axis=0, concat_axis=0, tiled=True)


def swap_back(array, parts):
    return lax.all_to_all(array, "seq", split_axis=0, concat_axis=0, tiled=True)


class Slice:
    def __init__(self, n_dp, n_seq):
        dp_bits, seq_bits = n_dp.bit_length() - 1, n_seq.bit_length() - 1
        dp = [("dp", i) for i in range(dp_bits)]
        seq = [("seq", i) for i in range(seq_bits)]
        even = dp[:1] + dp[1:2] + seq
        odd = dp[:1] + seq[:1] + dp[1:2] + seq[1:]
        self.plans = (even, odd)
        self.halvings = len(even)
        self.ways = 1 << max(dp_bits - 2, 0)
        self.bits = dp_bits + seq_bits
        self.pairs = []
        for stage in range(self.halvings):
            pairs = []
            for d in range(n_dp):
                for s in range(n_seq):
                    axis, i = self.plans[d & 1][stage]
                    to = (d ^ (1 << i), s) if axis == "dp" else (d, s ^ (1 << i))
                    pairs.append((d * n_seq + s, to[0] * n_seq + to[1]))
            self.pairs.append(pairs)
        self.far_pairs = [
            [(d, d ^ (k << 2)) for d in range(n_dp)] for k in range(self.ways)
        ]
        self.index = {"dp": lax.axis_index("dp"), "seq": lax.axis_index("seq")}
        self.core = self.index["dp"] & 1
        self.place = self.index["dp"] >> 2
        self.mine = [self.bit(stage, self.core) for stage in range(self.halvings)]

    def bit(self, stage, core):
        even, odd = [(self.index[axis] >> i) & 1 for axis, i in (p[stage] for p in self.plans)]
        return jnp.where(core == 0, even, odd)

    def swap(self, array, stage):
        return lax.ppermute(array, ("dp", "seq"), self.pairs[stage])

    def far_swap(self, array, k):
        return lax.ppermute(array, "dp", self.far_pairs[k])

    def places(self):
        result = []
        for core, half in ((self.core, self.mine[0]), (self.core ^ 1, self.mine[0] ^ 1)):
            low = 0
            for stage in range(1, self.halvings):
                low = low * 2 + self.bit(stage, core)
            result += [low * self.ways + self.place, half]
        return jnp.stack([jnp.asarray(v, jnp.int32) for v in result])

    def padded(self, rows):
        unit = max(16 << self.bits, 2 * TOKENS)
        return -(-rows // unit) * unit


def add_parts(rows, picks, keep, got):
    count, width = keep.shape[0] // rows, keep.shape[1]

    def kernel(picks_ref, keep_ref, got_ref, *out_refs):
        for i, out_ref in enumerate(out_refs):
            here = pl.ds(pl.multiple_of(picks_ref[i] * rows, rows), rows)
            out_ref[...] = (keep_ref[here, :].astype(F32) + got_ref[here, :].astype(F32)).astype(BF16)

    vmem = pl.BlockSpec(memory_space=pltpu.VMEM)
    return pl.pallas_call(
        kernel,
        in_specs=[pl.BlockSpec(memory_space=pltpu.SMEM), vmem, vmem],
        out_specs=[vmem] * count,
        out_shape=[jax.ShapeDtypeStruct((rows, width), BF16)] * count,
        compiler_params=pltpu.CompilerParams(vmem_limit_bytes=16 * 2**20),
        cost_estimate=cost(0, 6 * keep.size),
        name="add_parts",
    )(picks, keep, got)


class Table:
    def __init__(self, devices, send):
        self.devices = devices
        self.stage = 0
        self.keep = None
        self.sent = send
        self.got = devices.swap(send, 0)
        self.piece_rows = 2 * send.shape[0] >> devices.bits
        self.deps = [send]

    def advance(self, token=0):
        devices = self.devices
        last = devices.halvings
        self.stage += 1
        stage = self.stage
        if stage < last:
            bit = devices.mine[stage] + token
            keep, got = (a.reshape(2, -1, a.shape[1]) for a in (self.keep, self.got))

            def added(i):
                parts = [
                    lax.dynamic_index_in_dim(a, i, 0, keepdims=False).astype(F32)
                    for a in (keep, got)
                ]
                return (parts[0] + parts[1]).astype(BF16)

            self.sent, self.keep = added(1 - bit), added(bit)
            self.got = devices.swap(self.sent, stage)
            self.deps = [self.sent, self.keep]
        elif stage == last:
            place = devices.place + token
            picks = jnp.stack([place ^ k for k in range(devices.ways)])
            rows = self.keep.shape[0] // devices.ways
            self.keep, *self.sent = add_parts(rows, picks, self.keep, self.got)
            self.got = [devices.far_swap(a, k + 1) for k, a in enumerate(self.sent)]
            self.deps = [self.keep, *self.sent]
        elif stage == last + 1:
            total = self.keep.astype(F32)
            for a in self.got:
                total = total + a.astype(F32)
            if not isinstance(token, int):
                total = jnp.where(token == 0, total, 0.0)
            self.sent = total.astype(BF16)
            self.got = [devices.far_swap(self.sent, k) for k in range(1, devices.ways)]
            self.deps = [self.sent]
        else:
            got = self.got if isinstance(self.got, list) else [self.got]
            if not isinstance(token, int):
                got = [jnp.where(token == 0, a, self.sent) for a in got]
            self.sent = jnp.concatenate([self.sent, *got], axis=0)
            self.got = devices.swap(self.sent, 2 * last + 1 - stage)
            self.deps = [self.sent]
        return self.deps

    def finish(self):
        while self.stage < 2 * self.devices.halvings + 1:
            self.advance()
        return self.sent, self.got


def on_device(
    tokens, segment_ids, w_qkv, b_qv, w_out, b_out, gain_one, shift_one,
    w_inner, b_inner, w_final, b_final, gain_two, shift_two, out_grad,
):
    parts, local_len, width = tokens.shape
    hidden = w_inner.shape[1]
    length = parts * local_len
    x = swap_rows(tokens, parts).reshape(length, width)
    segments = swap_rows(segment_ids, parts).reshape(length, 1)
    grads_in = swap_rows(out_grad, parts).reshape(length, width)

    slot = jnp.arange(PAIR, dtype=jnp.int32)[None, :]
    same = segments == slot
    kext = jnp.where(same | ((slot >= NSEG) & (slot < NSEG + 3)), 1.0, 0.0).astype(BF16)
    qext = jnp.where(same | (slot >= NSEG), 0.0, -FAR).astype(BF16)

    def row(vector):
        return vector.astype(F32).reshape(1, -1)

    devices = Slice(lax.axis_size("dp"), lax.axis_size("seq"))
    bit = jnp.asarray(devices.mine[0], jnp.int32).reshape(1)
    q, k, v, context, lse, xt = forward_attention(
        x, kext, qext, w_qkv, row(b_qv[0]), row(b_qv[1])
    )
    vectors = [
        row(v_) for v_ in (b_out, gain_one, shift_one, b_inner, b_final, gain_two, shift_two)
    ]
    (
        own_out, other_out, pooled, low, hat, inverse, grad_two, grad_final, slope, dw_final, gb_two,
    ) = forward_dense(context, x, grads_in, kext, w_out, w_inner, w_final, vectors)
    sum_final = lax.psum_scatter(dw_final, ("dp", "seq"), scatter_dimension=0, tiled=True)
    if parts == 2:
        me = lax.axis_index("seq")
        got = lax.ppermute(other_out, "seq", [(0, 1), (1, 0)])
        output_block = jnp.where(me == 0, jnp.stack([own_out, got]), jnp.stack([got, own_out]))
        other = lax.ppermute(pooled, "seq", [(0, 1), (1, 0)])
        pooled_all = jnp.where(me == 0, jnp.stack([pooled, other]), jnp.stack([other, pooled]))
    else:
        output = jnp.concatenate([own_out, other_out], axis=0)
        output_block = swap_back(output.reshape(parts, local_len, width), parts)
        pooled_all = lax.all_gather(pooled, "seq", axis=0)
    resid_grad, grad_context, grad_inner, attended, gb_one, gb_inner, token = backward_dense(
        grad_final, slope, grad_two, hat, inverse, w_out, w_inner, w_final, row(gain_one), []
    )
    send, keep, token = dense_weights(
        bit, devices.padded(hidden + width + 32), low, grad_inner, context, attended,
        gb_one, gb_inner, gb_two, [output_block, pooled_all],
    )
    t_inner = Table(devices, send)
    t_inner.keep = keep
    heads = (q, k, v, grad_context, context)
    groups = width // GROUP
    qkv_rows = devices.padded(3 * width * groups + 8 * groups + 8)
    early, merged, biases = [], [], []
    for group in range(groups):
        last = group == groups - 1
        deps = t_inner.advance(token[0]) if group else t_inner.deps
        *found, token = backward_attention(
            group, bit, qkv_rows, biases if last else [], early if last else [],
            xt, kext, qext, lse, heads, deps,
        )
        merged.append(found[-1] if last else found[1])
        if not last:
            early.append(found[0])
            biases.append(found[2])
    t_qkv = Table(devices, found[0])
    t_qkv.keep = found[1]
    t_inner.advance(token[0])
    own_x, other_x, token = input_grad(resid_grad, merged, w_qkv)
    if parts == 2:
        got = lax.ppermute(other_x, "seq", [(0, 1), (1, 0)]).astype(F32)
        input_block = jnp.where(me == 0, jnp.stack([own_x, got]), jnp.stack([got, own_x]))
    else:
        grad_x = jnp.concatenate([own_x.astype(BF16), other_x], axis=0)
        input_block = swap_back(grad_x.reshape(parts, local_len, width), parts).astype(F32)
    t_qkv.advance(token[0])
    all_final = lax.all_gather(sum_final, ("dp", "seq"), axis=0, tiled=True)
    ends = [t.finish() for t in (t_qkv, t_inner)]
    places = devices.places()
    wide_final = turn(all_final, [input_block])
    wide_inner, wide_out, small = widen(
        widen_inner_kernel, t_inner.piece_rows, places, ends[1],
        [(width, hidden), (width, width), (32, width)], "widen_inner",
    )
    wide_qkv, small_qv = widen(
        widen_qkv_kernel, t_qkv.piece_rows, places, ends[0],
        [(width, 3 * width), (8 * groups + 8, GROUP)], "widen_qkv",
    )

    gb_qv = jnp.stack(
        [jnp.concatenate([small_qv[8 * g + j] for g in range(groups)]) for j in range(2)]
    )
    return (
        output_block,
        pooled_all,
        input_block,
        wide_qkv,
        gb_qv,
        wide_out,
        small[2],
        small[0],
        small[1],
        wide_inner,
        small[8 : 8 + hidden // width].reshape(-1),
        wide_final,
        small[18],
        small[16],
        small[17],
    )


def solution(mesh):
    rows = P("dp", "seq", None)
    return jax.shard_map(
        on_device,
        mesh=mesh,
        in_specs=(rows, P("dp", "seq")) + (P(),) * 12 + (rows,),
        out_specs=(rows, P("dp", None, None), rows) + (P(),) * 12,
        check_vma=False,
    )
```

```python
import math

import jax
import jax.numpy as jnp
from jax import lax
from jax.experimental import pallas as pl
from jax.experimental.pallas import tpu as pltpu
from jax.sharding import PartitionSpec as P

HEADS = 12
HEAD_DIM = 64
NSEG = 32
EPSILON = 1e-06
F32 = jnp.float32
BF16 = jnp.bfloat16
FAR = 1e30
PAIR = 2 * HEAD_DIM
GROUP = 2 * PAIR
QROWS = 256
KROWS = 512
TOKENS = 512
UNIT = 256
CHUNK = 768


def dot(a, b):
    return jnp.dot(a, b, preferred_element_type=F32)


def dot_nt(a, b):
    return lax.dot_general(a, b, (((1,), (1,)), ((), ())), preferred_element_type=F32)


def dot_tn(a, b):
    return lax.dot_general(a, b, (((0,), (0,)), ((), ())), preferred_element_type=F32)


def lanes(rows):
    return lax.broadcasted_iota(jnp.int32, (rows, PAIR), 1)


def whole(shape):
    zeros = (0,) * len(shape)
    return pl.BlockSpec(shape, lambda i: zeros, pipeline_mode=pl.Buffered(1))


def pad_rows(table, devices):
    return jnp.pad(table, ((0, devices.padded(table.shape[0]) - table.shape[0]), (0, 0)))


def rows_of(count, width):
    return pl.BlockSpec((count, width), lambda i: (i, 0))


def columns_of(count, width, offset=0):
    return pl.BlockSpec((count, width), lambda i: (0, i + offset))


def params(mib):
    return pltpu.CompilerParams(
        dimension_semantics=("arbitrary",), vmem_limit_bytes=mib * 2**20
    )


def cost(flops, nbytes, exps=0):
    return pl.CostEstimate(flops=flops, bytes_accessed=nbytes, transcendentals=exps)


def split_three(values):
    high = values.astype(BF16).astype(F32)
    rest = values - high
    middle = rest.astype(BF16).astype(F32)
    return high, middle, rest - middle


def in_lanes(lane, parts, other):
    high, middle, last = parts
    return jnp.where(
        lane == NSEG,
        high,
        jnp.where(lane == NSEG + 1, middle, jnp.where(lane == NSEG + 2, last, other)),
    )


def forward_attention_kernel(
    x_ref, kext_ref, qext_ref, wq_ref, wk_ref, wv_ref, bq_ref, bv_ref,
    q_ref, k_ref, v_ref, ctx_ref, lse_ref, xt_ref,
    qx, kx, vx,
):
    group = pl.program_id(0)
    length = x_ref.shape[0]
    xt_ref[...] = x_ref[:, pl.ds(pl.multiple_of(group * GROUP, GROUP), GROUP)].astype(F32).T.astype(BF16)
    x = x_ref[...]
    queries = (dot(x, wq_ref[...]) + bq_ref[...]).astype(BF16).astype(F32) * HEAD_DIM**-0.5
    keys = dot(x, wk_ref[...]).astype(BF16)
    values = (dot(x, wv_ref[...]) + bv_ref[...]).astype(BF16)
    q_ref[...] = queries.astype(BF16)
    k_ref[...] = keys
    v_ref[...] = values
    values = values.astype(F32)
    lane = lanes(length)
    for pair in range(2):
        part = slice(pair * PAIR, (pair + 1) * PAIR)
        kx[pair, :, :PAIR] = keys[:, part]
        kx[pair, :, PAIR:] = kext_ref[...]
        for half in range(2):
            mine = (lane // HEAD_DIM) == half
            qx[2 * pair + half, :, :PAIR] = jnp.where(mine, queries[:, part], 0.0).astype(BF16)
            qx[2 * pair + half, :, PAIR:] = qext_ref[...]
            vx[2 * pair + half] = jnp.where(mine, values[:, part], 1.0).astype(BF16)

    @pl.when(group == 0)
    def _():
        lse_ref[...] = jnp.zeros_like(lse_ref)

    lane = lanes(QROWS)

    def block(i, carry):
        rows = pl.ds(pl.multiple_of(i * QROWS, QROWS), QROWS)
        lse_all = lse_ref[rows, :]

        def scores_of(head):
            return dot_nt(qx[head, rows, :], kx[head // 2])

        ahead = scores_of(0)
        for pair in range(2):
            contexts = []
            for half in range(2):
                scores = ahead
                if 2 * pair + half < 3:
                    ahead = scores_of(2 * pair + half + 1)
                row_max = jnp.max(scores, axis=1, keepdims=True)
                weights = jnp.exp(scores - row_max).astype(BF16)
                sums = dot(weights, vx[2 * pair + half])
                at = (1 - half) * HEAD_DIM
                row_total = sums[:, at : at + 1]
                contexts.append(sums / row_total)
                lse_all = jnp.where(
                    lane == group * 4 + 2 * pair + half, row_max + jnp.log(row_total), lse_all
                )
            ctx_ref[rows, pair * PAIR : (pair + 1) * PAIR] = jnp.where(
                lane < HEAD_DIM, contexts[0], contexts[1]
            ).astype(BF16)
        lse_ref[rows, :] = lse_all
        return carry

    lax.fori_loop(0, length // QROWS, block, 0)


def forward_attention(x, kext, qext, w_qkv, bias_q, bias_v):
    length, width = x.shape
    groups = width // GROUP
    wide = jax.ShapeDtypeStruct((length, width), BF16)
    return pl.pallas_call(
        forward_attention_kernel,
        grid=(groups,),
        in_specs=[
            whole((length, width)),
            whole((length, PAIR)),
            whole((length, PAIR)),
            columns_of(width, GROUP),
            columns_of(width, GROUP, groups),
            columns_of(width, GROUP, 2 * groups),
            columns_of(1, GROUP),
            columns_of(1, GROUP),
        ],
        out_specs=[columns_of(length, GROUP)] * 4
        + [whole((length, PAIR)), rows_of(GROUP, length)],
        out_shape=[wide] * 4
        + [
            jax.ShapeDtypeStruct((length, PAIR), F32),
            jax.ShapeDtypeStruct((width, length), BF16),
        ],
        scratch_shapes=[
            pltpu.VMEM((4, length, 2 * PAIR), BF16),
            pltpu.VMEM((2, length, 2 * PAIR), BF16),
            pltpu.VMEM((4, length, PAIR), BF16),
        ],
        compiler_params=params(48),
        cost_estimate=cost(24 * 10**9, 16 * 10**6, HEADS * length * length),
        name="attention_forward",
    )(x, kext, qext, w_qkv, w_qkv, w_qkv, bias_q, bias_v)


def backward_attention_kernel(group, last, deps, bit_ref, *refs):
    (
        xt_ref, kext_ref, qext_ref, lse_ref, q_ref, k_ref, v_ref, go_ref, ctx_ref,
    ) = refs[:9]
    refs = refs[9 + deps :]
    if last:
        gb_refs, early_refs, refs = refs[:group], refs[group : 2 * group], refs[2 * group :]
        send_ref, keep_ref, merged, token, *refs = refs
    else:
        dw_ref, merged, gb_ref, token, *refs = refs
    qx, gx, kx, vx, kt, dk_acc, dv_acc = refs
    token[0] = 0
    length = q_ref.shape[0]
    width = xt_ref.shape[0]
    lane = lanes(length)
    for pair in range(2):
        part = slice(pair * PAIR, (pair + 1) * PAIR)
        keys = k_ref[:, part]
        kx[:, :PAIR] = keys
        kx[:, PAIR:] = kext_ref[...]
        vx[:, :PAIR] = v_ref[:, part]
        vx[:, PAIR:] = kext_ref[...]
        kt[...] = keys.astype(F32).T.astype(BF16)
        queries = q_ref[:, part].astype(F32)
        grads = go_ref[:, part].astype(F32)
        products = grads * ctx_ref[:, part].astype(F32)
        for half in range(2):
            mine = (lane // HEAD_DIM) == half
            head = group * 4 + 2 * pair + half
            lse = lse_ref[:, head : head + 1]
            delta = jnp.sum(jnp.where(mine, products, 0.0), axis=1, keepdims=True)
            qx[half, :, :PAIR] = jnp.where(mine, queries, 0.0).astype(BF16)
            qx[half, :, PAIR:] = in_lanes(
                lane, split_three(-lse), qext_ref[...].astype(F32)
            ).astype(BF16)
            gx[half, :, :PAIR] = jnp.where(mine, grads, 0.0).astype(BF16)
            gx[half, :, PAIR:] = in_lanes(lane, split_three(-delta), 0.0).astype(BF16)
        dk_acc[...] = jnp.zeros_like(dk_acc)
        dv_acc[...] = jnp.zeros_like(dv_acc)

        def block(i, carry):
            rows = pl.ds(pl.multiple_of(i * QROWS, QROWS), QROWS)
            units = [(half, k) for k in range(0, length, KROWS) for half in range(2)]
            grad_queries = [None, None]

            def products_of(half, k):
                return (
                    dot_nt(kx[k : k + KROWS, :], qx[half, rows, :]),
                    dot_nt(vx[k : k + KROWS, :], gx[half, rows, :]),
                )

            ahead = products_of(*units[0])
            for n, (half, k) in enumerate(units):
                scores, grad_prob = ahead
                if n + 1 < len(units):
                    ahead = products_of(*units[n + 1])
                prob = jnp.exp(scores)
                grad_score = (prob * grad_prob).astype(BF16)
                dv_acc[k : k + KROWS, :] += dot(prob.astype(BF16), gx[half, rows, :PAIR])
                dk_acc[k : k + KROWS, :] += dot(grad_score, qx[half, rows, :PAIR])
                found = dot(kt[half * HEAD_DIM : (half + 1) * HEAD_DIM, k : k + KROWS], grad_score)
                grad_queries[half] = found if k == 0 else grad_queries[half] + found
            merged[rows, part] = (
                jnp.concatenate(grad_queries, axis=0).T * HEAD_DIM**-0.5
            ).astype(BF16)
            return carry

        lax.fori_loop(0, length // QROWS, block, 0)
        merged[:, GROUP + pair * PAIR : GROUP + (pair + 1) * PAIR] = dk_acc[...].astype(BF16)
        merged[:, 2 * GROUP + pair * PAIR : 2 * GROUP + (pair + 1) * PAIR] = dv_acc[
            ...
        ].astype(BF16)

    bias, found = [], []
    for j in range(3):
        grads = merged[:, j * GROUP : (j + 1) * GROUP]
        if j != 1:
            bias.append(jnp.sum(grads.astype(F32), axis=0, keepdims=True))
        dw = dot(xt_ref[...], grads).astype(BF16)
        if last:
            found.append(dw)
        else:
            dw_ref[j * width : (j + 1) * width, :] = dw
    bias = jnp.concatenate(bias + [jnp.zeros((6, GROUP), F32)], axis=0)
    if not last:
        gb_ref[...] = bias
        return
    half = send_ref.shape[0]
    bias = jnp.concatenate([ref[...] for ref in gb_refs] + [bias, jnp.zeros_like(bias)], axis=0)
    found = list(early_refs) + found + [bias.astype(BF16)]
    filler = 2 * half - sum(values.shape[0] for values in found)
    if filler:
        found.append(jnp.zeros((filler, GROUP), BF16))

    def put(refs):
        at = 0
        for values in found:
            done = 0
            while done < values.shape[0]:
                which, row = (at + done) // half, (at + done) % half
                count = min(values.shape[0] - done, half - row)
                refs[which][row : row + count, :] = values[done : done + count, :]
                done += count
            at += values.shape[0]

    @pl.when(bit_ref[0] == 0)
    def _():
        put((keep_ref, send_ref))

    @pl.when(bit_ref[0] != 0)
    def _():
        put((send_ref, keep_ref))


def backward_attention(group, bit, rows, biases, early, xt, kext, qext, lse, heads, deps):
    width, length = xt.shape
    last = bool(biases)
    operands = [xt, kext, qext, lse, *heads, *deps, *biases, *early]
    in_specs = [
        whole((width, length)),
        whole((length, PAIR)),
        whole((length, PAIR)),
        whole((length, PAIR)),
    ]
    in_specs += [columns_of(length, GROUP, group)] * 5
    in_specs += [pl.BlockSpec(memory_space=pl.ANY)] * len(deps)
    in_specs += [whole((8, GROUP))] * len(biases) + [whole((3 * width, GROUP))] * len(early)
    shape = jax.ShapeDtypeStruct
    if last:
        outs = [((rows // 2, GROUP), BF16)] * 2 + [((length, 3 * GROUP), BF16)]
    else:
        outs = [((3 * width, GROUP), BF16), ((length, 3 * GROUP), BF16), ((8, GROUP), F32)]

    def kernel(*refs):
        backward_attention_kernel(group, last, len(deps), *refs)

    return pl.pallas_call(
        kernel,
        grid=(1,),
        in_specs=[pl.BlockSpec(memory_space=pltpu.SMEM)] + in_specs,
        out_specs=[whole(o[0]) for o in outs] + [pl.BlockSpec(memory_space=pltpu.SMEM)],
        scratch_shapes=[
            pltpu.VMEM((2, length, 2 * PAIR), BF16),
            pltpu.VMEM((2, length, 2 * PAIR), BF16),
            pltpu.VMEM((length, 2 * PAIR), BF16),
            pltpu.VMEM((length, 2 * PAIR), BF16),
            pltpu.VMEM((PAIR, length), BF16),
            pltpu.VMEM((length, PAIR), F32),
            pltpu.VMEM((length, PAIR), F32),
        ],
        out_shape=[shape(*o) for o in outs] + [shape((1,), jnp.int32)],
        compiler_params=params(48),
        cost_estimate=cost(8 * 10**9, 10 * 10**6, 4 * length * length),
        name="attention_backward",
    )(bit, *operands)


def input_grad_kernel(resid_ref, m0_ref, m1_ref, m2_ref, w_ref, *refs):
    own_ref, other_ref, token = refs[-3:]
    token[0] = 0
    width = resid_ref.shape[1]
    total = resid_ref[...]
    for group, merged in enumerate((m0_ref, m1_ref, m2_ref)):
        columns = [
            w_ref[:, j * width + group * GROUP : j * width + (group + 1) * GROUP] for j in range(3)
        ]
        total = total + dot_nt(merged[...], jnp.concatenate(columns, axis=1))
    step = pl.program_id(0)

    @pl.when(step < pl.num_programs(0) // 2)
    def _():
        own_ref[...] = total

    @pl.when(step >= pl.num_programs(0) // 2)
    def _():
        other_ref[...] = total.astype(BF16)


def input_grad(resid, merged, w_qkv, deps):
    length, width = resid.shape
    half = length // TOKENS // 2
    shape = jax.ShapeDtypeStruct
    return pl.pallas_call(
        input_grad_kernel,
        grid=(2 * half,),
        in_specs=[rows_of(TOKENS, width)]
        + [rows_of(TOKENS, 3 * GROUP)] * len(merged)
        + [whole(w_qkv.shape)]
        + [pl.BlockSpec(memory_space=pl.ANY)] * len(deps),
        out_specs=[
            pl.BlockSpec((TOKENS, width), lambda i: (jnp.minimum(i, half - 1), 0)),
            pl.BlockSpec((TOKENS, width), lambda i: (jnp.maximum(i - half, 0), 0)),
            pl.BlockSpec(memory_space=pltpu.SMEM),
        ],
        out_shape=[
            shape((length // 2, width), F32),
            shape((length // 2, width), BF16),
            shape((1,), jnp.int32),
        ],
        compiler_params=params(48),
        cost_estimate=cost(4 * 10**9, 16 * 10**6),
        name="input_grad",
    )(resid, *merged, w_qkv, *deps)


def normalize(values):
    centered = values - jnp.mean(values, axis=1, keepdims=True)
    inverse = lax.rsqrt(jnp.mean(centered * centered, axis=1, keepdims=True) + EPSILON)
    return centered * inverse, inverse


def normalize_back(grads, hat, inverse):
    return inverse * (
        grads
        - jnp.mean(grads, axis=1, keepdims=True)
        - hat * jnp.mean(grads * hat, axis=1, keepdims=True)
    )


def gelu_and_slope(values):
    cumulative = 0.5 + 0.5 * lax.erf(values * 0.7071067811865476)
    bell = jnp.exp2(values * values * -0.7213475204444817)
    return values * cumulative, cumulative + values * bell * 0.3989422804014327


def forward_dense_kernel(
    ctx_ref, x_ref, og_ref, kext_ref, w_out_ref, w_inner_ref, w_final_ref,
    b_out_ref, g_one_ref, s_one_ref, b_inner_ref, b_final_ref, g_two_ref, s_two_ref,
    own_ref, other_ref, pooled_ref, low_ref, hat_ref, inv_ref, grad_ref, final_ref, slope_ref, dw_ref, gb_ref,
    act, final, sums, counts, pre,
):
    step = pl.program_id(0)
    count, width = x_ref.shape
    hidden = w_inner_ref.shape[1]
    rows = pl.ds(pl.multiple_of(step * count, count), count)

    @pl.when(step == 0)
    def _():
        sums[...] = jnp.zeros_like(sums)
        counts[...] = jnp.zeros_like(counts)
        gb_ref[...] = jnp.zeros_like(gb_ref)

    resid = x_ref[...].astype(F32) + dot(ctx_ref[...], w_out_ref[...]) + b_out_ref[...]
    hat, inverse = normalize(resid)
    hat_ref[...] = hat
    inv_ref[...] = jnp.broadcast_to(inverse, inv_ref.shape)
    normed = hat * g_one_ref[...] + s_one_ref[...]
    low = normed.astype(BF16)
    low_ref[...] = normed.T.astype(BF16)
    total = normed + b_final_ref[...]

    def inner_of(c):
        part = slice(c * CHUNK, (c + 1) * CHUNK)
        pre[c % 2] = dot(low, w_inner_ref[:, part])

    inner_of(0)
    for c in range(hidden // CHUNK):
        if c + 1 < hidden // CHUNK:
            inner_of(c + 1)
        for r in range(0, count, 32):
            for j in range(0, CHUNK, GROUP):
                part = slice(c * CHUNK + j, c * CHUNK + j + GROUP)
                inner = pre[c % 2, r : r + 32, j : j + GROUP] + b_inner_ref[:, part]
                gelu, slope = gelu_and_slope(inner)
                slope_ref[r : r + 32, part] = slope.astype(BF16)
                act[pl.ds(pl.multiple_of(step * count + r, 32), 32), part] = gelu.astype(BF16)
        part = slice(c * CHUNK, (c + 1) * CHUNK)
        total = total + dot(act[rows, part], w_final_ref[part, :])
    hat, inverse = normalize(total)
    layer_out = hat * g_two_ref[...] + s_two_ref[...]
    high = layer_out.astype(BF16)

    @pl.when(step < pl.num_programs(0) // 2)
    def _():
        own_ref[...] = high

    @pl.when(step >= pl.num_programs(0) // 2)
    def _():
        other_ref[...] = high

    rest = (layer_out - high.astype(F32)).astype(BF16)
    member = kext_ref[...]
    sums[...] += dot_tn(member, high) + dot_tn(member, rest)
    counts[...] += dot_tn(member, jnp.ones((count, PAIR), BF16))
    grads = og_ref[...].astype(F32)
    gb_ref[0:1, :] += jnp.sum(grads * hat, axis=0, keepdims=True)
    gb_ref[1:2, :] += jnp.sum(grads, axis=0, keepdims=True)
    grads = normalize_back(grads * g_two_ref[...], hat, inverse)
    grad_ref[...] = grads
    grads = grads.astype(BF16)
    final_ref[...] = grads
    final[:, rows] = grads.astype(F32).T.astype(BF16)
    gb_ref[2:3, :] += jnp.sum(grads.astype(F32), axis=0, keepdims=True)

    @pl.when(step == pl.num_programs(0) - 1)
    def _():
        pooled_ref[...] = sums[:NSEG, :] / jnp.maximum(counts[:NSEG, :1], 1.0)


        def chunk(c, carry):
            here = pl.ds(pl.multiple_of(c * width, width), width)
            dw_ref[here, :] = dot(final[...], act[:, here]).astype(BF16)
            return carry

        lax.fori_loop(0, hidden // width, chunk, 0)


def forward_dense(context, x, out_grad, kext, w_out, w_inner, w_final, vectors):
    length, width = x.shape
    hidden = w_inner.shape[1]
    half = length // TOKENS // 2
    shape = jax.ShapeDtypeStruct
    return pl.pallas_call(
        forward_dense_kernel,
        grid=(length // TOKENS,),
        in_specs=[rows_of(TOKENS, width)] * 3
        + [rows_of(TOKENS, PAIR), whole(w_out.shape), whole(w_inner.shape), whole(w_final.shape)]
        + [whole(v.shape) for v in vectors],
        out_specs=[
            pl.BlockSpec((TOKENS, width), lambda i: (jnp.minimum(i, half - 1), 0)),
            pl.BlockSpec((TOKENS, width), lambda i: (jnp.maximum(i - half, 0), 0)),
            whole((NSEG, width)),
            columns_of(width, TOKENS),
            rows_of(TOKENS, width),
            rows_of(TOKENS, PAIR),
            rows_of(TOKENS, width),
            rows_of(TOKENS, width),
            rows_of(TOKENS, hidden),
            whole((hidden, width)),
            whole((8, width)),
        ],
        out_shape=[
            shape((length // 2, width), BF16),
            shape((length // 2, width), BF16),
            shape((NSEG, width), F32),
            shape((width, length), BF16),
            shape((length, width), F32),
            shape((length, PAIR), F32),
            shape((length, width), F32),
            shape((length, width), BF16),
            shape((length, hidden), BF16),
            shape((hidden, width), BF16),
            shape((8, width), F32),
        ],
        scratch_shapes=[
            pltpu.VMEM((length, hidden), BF16),
            pltpu.VMEM((width, length), BF16),
            pltpu.VMEM((PAIR, width), F32),
            pltpu.VMEM((PAIR, PAIR), F32),
            pltpu.VMEM((2, TOKENS, CHUNK), F32),
        ],
        compiler_params=params(56),
        cost_estimate=cost(45 * 10**9, 45 * 10**6, length * hidden),
        name="dense_forward",
    )(context, x, out_grad, kext, w_out, w_inner, w_final, *vectors)


def backward_dense_kernel(deps, *refs):
    (
        final_ref, slope_ref, grad_ref, hat_ref, inv_ref,
        w_out_ref, w_inner_ref, w_final_ref, g_one_ref,
    ) = refs[:9]
    resid_ref, go_ref, inner_ref, attended_ref, gb_ref, gbi_ref, token = refs[9 + deps :]
    token[0] = 0
    step = pl.program_id(0)
    width = grad_ref.shape[1]
    hidden = w_inner_ref.shape[1]

    @pl.when(step == 0)
    def _():
        gb_ref[...] = jnp.zeros_like(gb_ref)
        gbi_ref[...] = jnp.zeros_like(gbi_ref)

    grads = grad_ref[...]
    for c in range(hidden // width):
        part = slice(c * width, (c + 1) * width)
        grad_act = dot_nt(final_ref[...], w_final_ref[part, :])
        grad_inner = (grad_act * slope_ref[:, part].astype(F32)).astype(BF16)
        inner_ref[:, part] = grad_inner
        gbi_ref[c : c + 1, :] += jnp.sum(grad_inner.astype(F32), axis=0, keepdims=True)
        grads = grads + dot_nt(grad_inner, w_inner_ref[:, part])
    hat = hat_ref[...]
    gb_ref[0:1, :] += jnp.sum(grads * hat, axis=0, keepdims=True)
    gb_ref[1:2, :] += jnp.sum(grads, axis=0, keepdims=True)
    grads = normalize_back(grads * g_one_ref[...], hat, inv_ref[:, :1])
    resid_ref[...] = grads
    low = grads.astype(BF16)
    gb_ref[2:3, :] += jnp.sum(low.astype(F32), axis=0, keepdims=True)
    attended_ref[...] = low
    go_ref[...] = dot_nt(low, w_out_ref[...]).astype(BF16)


def backward_dense(final, slope, grad_two, hat, inverse, w_out, w_inner, w_final, gain, deps):
    length, width = hat.shape
    hidden = w_inner.shape[1]
    shape = jax.ShapeDtypeStruct

    def kernel(*refs):
        backward_dense_kernel(len(deps), *refs)

    return pl.pallas_call(
        kernel,
        grid=(length // TOKENS,),
        in_specs=[
            rows_of(TOKENS, width),
            rows_of(TOKENS, hidden),
            rows_of(TOKENS, width),
            rows_of(TOKENS, width),
            rows_of(TOKENS, PAIR),
            whole(w_out.shape),
            whole(w_inner.shape),
            whole(w_final.shape),
            whole(gain.shape),
        ]
        + [pl.BlockSpec(memory_space=pl.ANY)] * len(deps),
        out_specs=[
            rows_of(TOKENS, width),
            rows_of(TOKENS, width),
            rows_of(TOKENS, hidden),
            rows_of(TOKENS, width),
            whole((8, width)),
            whole((8, width)),
            pl.BlockSpec(memory_space=pltpu.SMEM),
        ],
        out_shape=[
            shape((length, width), F32),
            shape((length, width), BF16),
            shape((length, hidden), BF16),
            shape((length, width), BF16),
            shape((8, width), F32),
            shape((8, width), F32),
            shape((1,), jnp.int32),
        ],
        compiler_params=params(56),
        cost_estimate=cost(8 * 10**9, 20 * 10**6),
        name="dense_backward",
    )(final, slope, grad_two, hat, inverse, w_out, w_inner, w_final, gain, *deps)


def dense_weights_kernel(deps, bit_ref, *refs):
    low_ref, inner_ref, ctx_ref, attended_ref, one_ref, bi_ref, two_ref = refs[:7]
    send_ref, keep_ref, token, dw_ref = refs[-4:]
    token[0] = 0
    step = pl.program_id(0)
    width = attended_ref.shape[1]
    last = pl.num_programs(0) - 1

    @pl.when(step < last)
    def _():
        here = pl.ds(pl.multiple_of(step * width, width), width)
        dw_ref[here, :] = dot(low_ref[...], inner_ref[...]).astype(BF16)

    @pl.when(step == last)
    def _():
        at = bi_ref.shape[0] // 2 * width
        dw_ref[at : at + width, :] = dot_tn(ctx_ref[...], attended_ref[...]).astype(BF16)
        at += width
        blocks = [one_ref[...], bi_ref[...], two_ref[...]]
        blocks.append(jnp.zeros((8, width), F32))
        dw_ref[at : at + 32, :] = jnp.concatenate(blocks, axis=0).astype(BF16)
        dw_ref[at + 32 :, :] = jnp.zeros_like(dw_ref[at + 32 :, :])
        half = send_ref.shape[0]
        send_ref[...] = dw_ref[pl.ds(pl.multiple_of((1 - bit_ref[0]) * half, half), half), :]
        keep_ref[...] = dw_ref[pl.ds(pl.multiple_of(bit_ref[0] * half, half), half), :]


def dense_weights(bit, rows, low, inner, context, attended, gb_one, gb_inner, gb_two, deps):
    width, length = low.shape
    hidden = inner.shape[1]
    blocks = hidden // width

    def kernel(*refs):
        dense_weights_kernel(len(deps), *refs)

    return pl.pallas_call(
        kernel,
        grid=(blocks + 1,),
        in_specs=[
            pl.BlockSpec(memory_space=pltpu.SMEM),
            whole((width, length)),
            pl.BlockSpec((length, width), lambda i: (0, jnp.minimum(i, blocks - 1))),
            whole((length, width)),
            whole((length, width)),
            whole((8, width)),
            whole((8, width)),
            whole((8, width)),
        ]
        + [pl.BlockSpec(memory_space=pl.ANY)] * len(deps),
        out_specs=[whole((rows // 2, width))] * 2 + [pl.BlockSpec(memory_space=pltpu.SMEM)],
        out_shape=[jax.ShapeDtypeStruct((rows // 2, width), BF16)] * 2
        + [jax.ShapeDtypeStruct((1,), jnp.int32)],
        scratch_shapes=[pltpu.VMEM((rows, width), BF16)],
        compiler_params=params(48),
        cost_estimate=cost(6 * 10**9, 16 * 10**6),
        name="dense_weights",
    )(bit, low, inner, context, attended, gb_one, gb_inner, gb_two, *deps)


def spread(own_ref, other_ref, scalars, rows, block, put):
    half = own_ref.shape[0]

    def move(ref, low, which):
        for piece in range(half // rows):
            start = which * half + piece * rows
            at = 0
            while at < rows:
                count = min(rows - at, block - (start + at) % block)
                here = pl.ds(pl.multiple_of((piece ^ low) * rows + at, math.gcd(rows, block)), count)
                put(start + at, ref[here, :].astype(F32))
                at += count

    for i, ref in enumerate((own_ref, other_ref)):
        for which in range(2):

            @pl.when(scalars[2 * i + 1] == which)
            def _():
                move(ref, scalars[2 * i], which)


def put_small(small_ref, row, values):
    count = min(values.shape[0], small_ref.shape[0] - row)
    if count > 0:
        small_ref[row : row + count, :] = values[:count, :]


def widen_inner_kernel(order, table_ref, inner_ref, out_ref, small_ref):
    width, hidden = inner_ref.shape
    rows = table_ref.shape[0] // len(order)
    for piece, device in enumerate(order):
        at = 0
        while at < rows:
            start = piece * rows + at
            count = min(rows - at, width - start % width)
            here = table_ref[device * rows + at : device * rows + at + count, :].astype(F32)
            block, row = start // width, start % width
            if start < hidden:
                inner_ref[row : row + count, block * width : (block + 1) * width] = here
            elif start < hidden + width:
                out_ref[row : row + count, :] = here
            else:
                put_small(small_ref, start - hidden - width, here)
            at += count


def widen_inner(order, table, hidden):
    width = table.shape[1]
    vmem = pl.BlockSpec(memory_space=pltpu.VMEM)
    shapes = [(width, hidden), (width, width), (32, width)]
    return pl.pallas_call(
        lambda *refs: widen_inner_kernel(order, *refs),
        in_specs=[vmem],
        out_specs=[vmem] * 3,
        out_shape=[jax.ShapeDtypeStruct(s, F32) for s in shapes],
        compiler_params=pltpu.CompilerParams(vmem_limit_bytes=40 * 2**20),
        cost_estimate=cost(0, 6 * table.size),
        name="widen_inner",
    )(table)


def turn_kernel(low_ref, *refs):
    refs[-1][0] = 0
    refs[-2][...] = low_ref[...].astype(F32).T


def turn(table, deps):
    rows, width = table.shape
    per = width // UNIT
    return pl.pallas_call(
        turn_kernel,
        grid=(rows // width, per),
        in_specs=[pl.BlockSpec((width, UNIT), lambda b, r: (b, r))]
        + [pl.BlockSpec(memory_space=pl.ANY)] * len(deps),
        out_specs=[
            pl.BlockSpec((UNIT, width), lambda b, r: (b * per + r, 0)),
            pl.BlockSpec(memory_space=pltpu.SMEM),
        ],
        out_shape=[
            jax.ShapeDtypeStruct((rows, width), F32),
            jax.ShapeDtypeStruct((1,), jnp.int32),
        ],
        cost_estimate=cost(0, 6 * rows * width),
        name="turn",
    )(table, *deps)


def widen_qkv_kernel(rows, scalars, own_ref, other_ref, out_ref, small_ref):
    width = out_ref.shape[0]

    def put(at, values):
        block, row = at // width, at % width
        if block < out_ref.shape[1] // GROUP:
            column = (block % 3) * width + (block // 3) * GROUP
            out_ref[row : row + values.shape[0], column : column + GROUP] = values
        else:
            put_small(small_ref, row + (block - out_ref.shape[1] // GROUP) * width, values)

    spread(own_ref, other_ref, scalars, rows, width, put)


def widen(kernel, rows, scalars, arrays, shapes, name):
    nbytes = sum(2 * a.size for a in arrays) + sum(4 * math.prod(s) for s in shapes)
    return pl.pallas_call(
        lambda *refs: kernel(rows, *refs),
        in_specs=[pl.BlockSpec(memory_space=pltpu.SMEM)]
        + [pl.BlockSpec(memory_space=pltpu.VMEM)] * len(arrays),
        out_specs=[pl.BlockSpec(memory_space=pltpu.VMEM)] * len(shapes),
        out_shape=[jax.ShapeDtypeStruct(s, F32) for s in shapes],
        compiler_params=pltpu.CompilerParams(vmem_limit_bytes=48 * 2**20),
        cost_estimate=cost(0, nbytes),
        name=name,
    )(scalars, *arrays)


def swap_rows(array, parts):
    if parts == 2:
        me = lax.axis_index("seq")
        own = lax.dynamic_index_in_dim(array, me, 0, keepdims=True)
        other = lax.dynamic_index_in_dim(array, 1 - me, 0, keepdims=True)
        got = lax.ppermute(other, "seq", [(0, 1), (1, 0)])
        return jnp.concatenate([own, got], axis=0)
    return lax.all_to_all(array, "seq", split_axis=0, concat_axis=0, tiled=True)


def swap_back(array, parts):
    return lax.all_to_all(array, "seq", split_axis=0, concat_axis=0, tiled=True)


class Slice:
    def __init__(self, n_dp, n_seq):
        dp_bits, seq_bits = n_dp.bit_length() - 1, n_seq.bit_length() - 1
        dp = [("dp", i) for i in range(dp_bits)]
        seq = [("seq", i) for i in range(seq_bits)]
        even = dp[:1] + dp[1:2] + seq
        odd = dp[:1] + seq[:1] + dp[1:2] + seq[1:]
        self.plans = (even, odd)
        self.halvings = len(even)
        self.ways = 1 << max(dp_bits - 2, 0)
        self.bits = dp_bits + seq_bits
        self.pairs = []
        for stage in range(self.halvings):
            pairs = []
            for d in range(n_dp):
                for s in range(n_seq):
                    axis, i = self.plans[d & 1][stage]
                    to = (d ^ (1 << i), s) if axis == "dp" else (d, s ^ (1 << i))
                    pairs.append((d * n_seq + s, to[0] * n_seq + to[1]))
            self.pairs.append(pairs)
        self.far_pairs = [
            [(d, d ^ (k << 2)) for d in range(n_dp)] for k in range(self.ways)
        ]
        self.index = {"dp": lax.axis_index("dp"), "seq": lax.axis_index("seq")}
        self.core = self.index["dp"] & 1
        self.place = self.index["dp"] >> 2
        self.mine = [self.bit(stage, self.core) for stage in range(self.halvings)]

    def bit(self, stage, core):
        even, odd = [(self.index[axis] >> i) & 1 for axis, i in (p[stage] for p in self.plans)]
        return jnp.where(core == 0, even, odd)

    def swap(self, array, stage):
        return lax.ppermute(array, ("dp", "seq"), self.pairs[stage])

    def far_swap(self, array, k):
        return lax.ppermute(array, "dp", self.far_pairs[k])

    def places(self):
        result = []
        for core, half in ((self.core, self.mine[0]), (self.core ^ 1, self.mine[0] ^ 1)):
            low = 0
            for stage in range(1, self.halvings):
                low = low * 2 + self.bit(stage, core)
            result += [low * self.ways + self.place, half]
        return jnp.stack([jnp.asarray(v, jnp.int32) for v in result])

    def owners(self, n_dp, n_seq):
        result = {}
        for d in range(n_dp):
            for s in range(n_seq):
                piece = 0
                for axis, i in self.plans[d & 1]:
                    piece = piece * 2 + (((d if axis == "dp" else s) >> i) & 1)
                result[piece * self.ways + (d >> 2)] = d * n_seq + s
        return [result[piece] for piece in range(n_dp * n_seq)]

    def padded(self, rows):
        unit = max(16 << self.bits, 2 * UNIT)
        return -(-rows // unit) * unit


def add_parts(rows, picks, keep, got, deps):
    count, width = keep.shape[0] // rows, keep.shape[1]

    def kernel(picks_ref, keep_ref, got_ref, *refs):
        refs[-1][0] = 0
        for i, out_ref in enumerate(refs[len(deps) : -1]):
            here = pl.ds(pl.multiple_of(picks_ref[i] * rows, rows), rows)
            out_ref[...] = (keep_ref[here, :].astype(F32) + got_ref[here, :].astype(F32)).astype(BF16)

    vmem = pl.BlockSpec(memory_space=pltpu.VMEM)
    smem = pl.BlockSpec(memory_space=pltpu.SMEM)
    return pl.pallas_call(
        kernel,
        in_specs=[smem, vmem, vmem] + [pl.BlockSpec(memory_space=pl.ANY)] * len(deps),
        out_specs=[vmem] * count + [smem],
        out_shape=[jax.ShapeDtypeStruct((rows, width), BF16)] * count
        + [jax.ShapeDtypeStruct((1,), jnp.int32)],
        compiler_params=pltpu.CompilerParams(vmem_limit_bytes=16 * 2**20),
        cost_estimate=cost(0, 6 * keep.size),
        name="add_parts",
    )(picks, keep, got, *deps)


class Table:
    def __init__(self, devices, send):
        self.devices = devices
        self.stage = 0
        self.keep = None
        self.sent = send
        self.got = devices.swap(send, 0)
        self.piece_rows = 2 * send.shape[0] >> devices.bits
        self.deps = [send]

    def advance(self, token=0, needs=()):
        devices = self.devices
        last = devices.halvings
        self.stage += 1
        stage = self.stage
        if stage < last:
            bit = devices.mine[stage] + token
            keep, got = (a.reshape(2, -1, a.shape[1]) for a in (self.keep, self.got))

            def added(i):
                parts = [
                    lax.dynamic_index_in_dim(a, i, 0, keepdims=False).astype(F32)
                    for a in (keep, got)
                ]
                return (parts[0] + parts[1]).astype(BF16)

            self.sent, self.keep = added(1 - bit), added(bit)
            self.got = devices.swap(self.sent, stage)
            self.deps = [self.sent, self.keep]
        elif stage == last:
            place = devices.place + token
            picks = jnp.stack([place ^ k for k in range(devices.ways)])
            rows = self.keep.shape[0] // devices.ways
            self.keep, *self.sent, self.token = add_parts(
                rows, picks, self.keep, self.got, list(needs)
            )
            self.got = [devices.far_swap(a, k + 1) for k, a in enumerate(self.sent)]
            self.deps = [self.keep, *self.sent]
        elif stage == last + 1:
            self.sent = self.total(token)
            self.got = [devices.far_swap(self.sent, k) for k in range(1, devices.ways)]
            self.deps = [self.sent]
        else:
            got = self.got if isinstance(self.got, list) else [self.got]
            if not isinstance(token, int):
                got = [jnp.where(token == 0, a, self.sent) for a in got]
            self.sent = jnp.concatenate([self.sent, *got], axis=0)
            self.got = devices.swap(self.sent, 2 * last + 1 - stage)
            self.deps = [self.sent]
        return self.deps

    def total(self, token):
        total = self.keep.astype(F32)
        for a in self.got:
            total = total + a.astype(F32)
        if not isinstance(token, int):
            total = jnp.where(token == 0, total, 0.0)
        return total.astype(BF16)

    def finish(self):
        while self.stage < 2 * self.devices.halvings + 1:
            self.advance()
        return self.sent, self.got


def on_device(
    tokens, segment_ids, w_qkv, b_qv, w_out, b_out, gain_one, shift_one,
    w_inner, b_inner, w_final, b_final, gain_two, shift_two, out_grad,
):
    parts, local_len, width = tokens.shape
    hidden = w_inner.shape[1]
    length = parts * local_len
    x = swap_rows(tokens, parts).reshape(length, width)
    segments = swap_rows(segment_ids, parts).reshape(length, 1)
    grads_in = swap_rows(out_grad, parts).reshape(length, width)

    slot = jnp.arange(PAIR, dtype=jnp.int32)[None, :]
    same = segments == slot
    kext = jnp.where(same | ((slot >= NSEG) & (slot < NSEG + 3)), 1.0, 0.0).astype(BF16)
    qext = jnp.where(same | (slot >= NSEG), 0.0, -FAR).astype(BF16)

    def row(vector):
        return vector.astype(F32).reshape(1, -1)

    devices = Slice(lax.axis_size("dp"), lax.axis_size("seq"))
    bit = jnp.asarray(devices.mine[0], jnp.int32).reshape(1)
    q, k, v, context, lse, xt = forward_attention(
        x, kext, qext, w_qkv, row(b_qv[0]), row(b_qv[1])
    )
    vectors = [
        row(v_) for v_ in (b_out, gain_one, shift_one, b_inner, b_final, gain_two, shift_two)
    ]
    (
        own_out, other_out, pooled, low, hat, inverse, grad_two, grad_final, slope, dw_final,
        gb_two,
    ) = forward_dense(
        context, x, grads_in, kext, w_out, w_inner, w_final, vectors
    )
    sum_final = lax.psum_scatter(dw_final, ("dp", "seq"), scatter_dimension=0, tiled=True)
    if parts == 2:
        me = lax.axis_index("seq")
        got = lax.ppermute(other_out, "seq", [(0, 1), (1, 0)])
        output_block = jnp.where(me == 0, jnp.stack([own_out, got]), jnp.stack([got, own_out]))
        other = lax.ppermute(pooled, "seq", [(0, 1), (1, 0)])
        pooled_all = jnp.where(me == 0, jnp.stack([pooled, other]), jnp.stack([other, pooled]))
    else:
        output = jnp.concatenate([own_out, other_out], axis=0)
        output_block = swap_back(output.reshape(parts, local_len, width), parts)
        pooled_all = lax.all_gather(pooled, "seq", axis=0)
    resid_grad, grad_context, grad_inner, attended, gb_one, gb_inner, token = backward_dense(
        grad_final, slope, grad_two, hat, inverse, w_out, w_inner, w_final, row(gain_one),
        [],
    )
    send, keep, token = dense_weights(
        bit, devices.padded(hidden + width + 32), low, grad_inner, context, attended,
        gb_one, gb_inner, gb_two, [output_block, pooled_all],
    )
    t_inner = Table(devices, send)
    t_inner.keep = keep
    heads = (q, k, v, grad_context, context)
    groups = width // GROUP
    qkv_rows = devices.padded(3 * width * groups + 8 * groups + 8)
    early, merged, biases = [], [], []
    for group in range(groups):
        last = group == groups - 1
        deps = t_inner.advance(token[0]) if group else t_inner.deps
        *found, token = backward_attention(
            group, bit, qkv_rows, biases if last else [], early if last else [],
            xt, kext, qext, lse, heads, deps,
        )
        merged.append(found[-1] if last else found[1])
        if not last:
            early.append(found[0])
            biases.append(found[2])
    t_qkv = Table(devices, found[0])
    t_qkv.keep = found[1]
    sum_final = jnp.where(token[0] == 0, sum_final, 0)
    all_final = lax.all_gather(sum_final, ("dp", "seq"), axis=0, tiled=True)
    own_x, other_x, token = input_grad(resid_grad, merged, w_qkv, [])
    while t_inner.stage < devices.halvings:
        t_inner.advance(token[0])
    if parts == 2:
        got = lax.ppermute(other_x, "seq", [(0, 1), (1, 0)]).astype(F32)
        input_block = jnp.where(me == 0, jnp.stack([own_x, got]), jnp.stack([got, own_x]))
    else:
        grad_x = jnp.concatenate([own_x.astype(BF16), other_x], axis=0)
        input_block = swap_back(grad_x.reshape(parts, local_len, width), parts).astype(F32)
    t_qkv.advance(token[0])
    while t_qkv.stage < devices.halvings:
        t_qkv.advance()
    sum_inner = t_inner.total(t_qkv.token[0])
    all_inner = lax.all_gather(sum_inner, ("dp", "seq"), axis=0, tiled=True)
    places = devices.places()
    wide_final, token = turn(all_final, [input_block])
    t_qkv.advance()
    t_qkv.advance(token[0])
    wide_qkv, small_qv = widen(
        widen_qkv_kernel, t_qkv.piece_rows, places, t_qkv.finish(),
        [(width, 3 * width), (8 * groups + 8, GROUP)], "widen_qkv",
    )
    order = devices.owners(lax.axis_size("dp"), lax.axis_size("seq"))
    wide_inner, wide_out, small = widen_inner(order, all_inner, hidden)

    gb_qv = jnp.stack(
        [jnp.concatenate([small_qv[8 * g + j] for g in range(groups)]) for j in range(2)]
    )
    return (
        output_block,
        pooled_all,
        input_block,
        wide_qkv,
        gb_qv,
        wide_out,
        small[2],
        small[0],
        small[1],
        wide_inner,
        small[8 : 8 + hidden // width].reshape(-1),
        wide_final,
        small[18],
        small[16],
        small[17],
    )


def solution(mesh):
    rows = P("dp", "seq", None)
    return jax.shard_map(
        on_device,
        mesh=mesh,
        in_specs=(rows, P("dp", "seq")) + (P(),) * 12 + (rows,),
        out_specs=(rows, P("dp", None, None), rows) + (P(),) * 12,
        check_vma=False,
    )
```

```python
import math

import jax
import jax.numpy as jnp
from jax import lax
from jax.experimental import pallas as pl
from jax.experimental.pallas import tpu as pltpu
from jax.sharding import PartitionSpec as P

HEADS = 12
HEAD_DIM = 64
NSEG = 32
EPSILON = 1e-06
F32 = jnp.float32
BF16 = jnp.bfloat16
FAR = 1e30
PAIR = 2 * HEAD_DIM
GROUP = 2 * PAIR
QROWS = 256
KROWS = 512
TOKENS = 512
UNIT = 256
CHUNK = 768


def dot(a, b):
    return jnp.dot(a, b, preferred_element_type=F32)


def dot_nt(a, b):
    return lax.dot_general(a, b, (((1,), (1,)), ((), ())), preferred_element_type=F32)


def dot_tn(a, b):
    return lax.dot_general(a, b, (((0,), (0,)), ((), ())), preferred_element_type=F32)


def lanes(rows):
    return lax.broadcasted_iota(jnp.int32, (rows, PAIR), 1)


def whole(shape):
    zeros = (0,) * len(shape)
    return pl.BlockSpec(shape, lambda i: zeros, pipeline_mode=pl.Buffered(1))


def pad_rows(table, devices):
    return jnp.pad(table, ((0, devices.padded(table.shape[0]) - table.shape[0]), (0, 0)))


def rows_of(count, width):
    return pl.BlockSpec((count, width), lambda i: (i, 0))


def columns_of(count, width, offset=0):
    return pl.BlockSpec((count, width), lambda i: (0, i + offset))


def params(mib):
    return pltpu.CompilerParams(
        dimension_semantics=("arbitrary",), vmem_limit_bytes=mib * 2**20
    )


def cost(flops, nbytes, exps=0):
    return pl.CostEstimate(flops=flops, bytes_accessed=nbytes, transcendentals=exps)


def split_three(values):
    high = values.astype(BF16).astype(F32)
    rest = values - high
    middle = rest.astype(BF16).astype(F32)
    return high, middle, rest - middle


def in_lanes(lane, parts, other):
    high, middle, last = parts
    return jnp.where(
        lane == NSEG,
        high,
        jnp.where(lane == NSEG + 1, middle, jnp.where(lane == NSEG + 2, last, other)),
    )


def forward_attention_kernel(
    x_ref, kext_ref, qext_ref, wq_ref, wk_ref, wv_ref, bq_ref, bv_ref,
    q_ref, k_ref, v_ref, ctx_ref, lse_ref, xt_ref,
    qx, kx, vx,
):
    group = pl.program_id(0)
    length = x_ref.shape[0]
    xt_ref[...] = x_ref[:, pl.ds(pl.multiple_of(group * GROUP, GROUP), GROUP)].astype(F32).T.astype(BF16)
    x = x_ref[...]
    queries = (dot(x, wq_ref[...]) + bq_ref[...]).astype(BF16).astype(F32) * HEAD_DIM**-0.5
    keys = dot(x, wk_ref[...]).astype(BF16)
    values = (dot(x, wv_ref[...]) + bv_ref[...]).astype(BF16)
    q_ref[...] = queries.astype(BF16)
    k_ref[...] = keys
    v_ref[...] = values
    values = values.astype(F32)
    lane = lanes(length)
    for pair in range(2):
        part = slice(pair * PAIR, (pair + 1) * PAIR)
        kx[pair, :, :PAIR] = keys[:, part]
        kx[pair, :, PAIR:] = kext_ref[...]
        for half in range(2):
            mine = (lane // HEAD_DIM) == half
            qx[2 * pair + half, :, :PAIR] = jnp.where(mine, queries[:, part], 0.0).astype(BF16)
            qx[2 * pair + half, :, PAIR:] = qext_ref[...]
            vx[2 * pair + half] = jnp.where(mine, values[:, part], 1.0).astype(BF16)

    @pl.when(group == 0)
    def _():
        lse_ref[...] = jnp.zeros_like(lse_ref)

    lane = lanes(QROWS)

    def block(i, carry):
        rows = pl.ds(pl.multiple_of(i * QROWS, QROWS), QROWS)
        lse_all = lse_ref[rows, :]

        def scores_of(head):
            return dot_nt(qx[head, rows, :], kx[head // 2])

        ahead = scores_of(0)
        for pair in range(2):
            contexts = []
            for half in range(2):
                scores = ahead
                if 2 * pair + half < 3:
                    ahead = scores_of(2 * pair + half + 1)
                row_max = jnp.max(scores, axis=1, keepdims=True)
                weights = jnp.exp(scores - row_max).astype(BF16)
                sums = dot(weights, vx[2 * pair + half])
                at = (1 - half) * HEAD_DIM
                row_total = sums[:, at : at + 1]
                contexts.append(sums / row_total)
                lse_all = jnp.where(
                    lane == group * 4 + 2 * pair + half, row_max + jnp.log(row_total), lse_all
                )
            ctx_ref[rows, pair * PAIR : (pair + 1) * PAIR] = jnp.where(
                lane < HEAD_DIM, contexts[0], contexts[1]
            ).astype(BF16)
        lse_ref[rows, :] = lse_all
        return carry

    lax.fori_loop(0, length // QROWS, block, 0)


def forward_attention(x, kext, qext, w_qkv, bias_q, bias_v):
    length, width = x.shape
    groups = width // GROUP
    wide = jax.ShapeDtypeStruct((length, width), BF16)
    return pl.pallas_call(
        forward_attention_kernel,
        grid=(groups,),
        in_specs=[
            whole((length, width)),
            whole((length, PAIR)),
            whole((length, PAIR)),
            columns_of(width, GROUP),
            columns_of(width, GROUP, groups),
            columns_of(width, GROUP, 2 * groups),
            columns_of(1, GROUP),
            columns_of(1, GROUP),
        ],
        out_specs=[columns_of(length, GROUP)] * 4
        + [whole((length, PAIR)), rows_of(GROUP, length)],
        out_shape=[wide] * 4
        + [
            jax.ShapeDtypeStruct((length, PAIR), F32),
            jax.ShapeDtypeStruct((width, length), BF16),
        ],
        scratch_shapes=[
            pltpu.VMEM((4, length, 2 * PAIR), BF16),
            pltpu.VMEM((2, length, 2 * PAIR), BF16),
            pltpu.VMEM((4, length, PAIR), BF16),
        ],
        compiler_params=params(60),
        cost_estimate=cost(24 * 10**9, 16 * 10**6, HEADS * length * length),
        name="attention_forward",
    )(x, kext, qext, w_qkv, w_qkv, w_qkv, bias_q, bias_v)


def backward_attention_kernel(group, last, deps, bit_ref, *refs):
    (
        xt_ref, kext_ref, qext_ref, lse_ref, q_ref, k_ref, v_ref, go_ref, ctx_ref,
    ) = refs[:9]
    refs = refs[9 + deps :]
    if last:
        gb_refs, early_refs, refs = refs[:group], refs[group : 2 * group], refs[2 * group :]
        send_ref, keep_ref, merged, token, *refs = refs
    else:
        dw_ref, merged, gb_ref, token, *refs = refs
    qx, gx, kx, vx, kt, dk_acc, dv_acc = refs
    token[0] = 0
    length = q_ref.shape[0]
    width = xt_ref.shape[0]
    lane = lanes(length)
    for pair in range(2):
        part = slice(pair * PAIR, (pair + 1) * PAIR)
        keys = k_ref[:, part]
        kx[:, :PAIR] = keys
        kx[:, PAIR:] = kext_ref[...]
        vx[:, :PAIR] = v_ref[:, part]
        vx[:, PAIR:] = kext_ref[...]
        kt[...] = keys.astype(F32).T.astype(BF16)
        queries = q_ref[:, part].astype(F32)
        grads = go_ref[:, part].astype(F32)
        products = grads * ctx_ref[:, part].astype(F32)
        for half in range(2):
            mine = (lane // HEAD_DIM) == half
            head = group * 4 + 2 * pair + half
            lse = lse_ref[:, head : head + 1]
            delta = jnp.sum(jnp.where(mine, products, 0.0), axis=1, keepdims=True)
            qx[half, :, :PAIR] = jnp.where(mine, queries, 0.0).astype(BF16)
            qx[half, :, PAIR:] = in_lanes(
                lane, split_three(-lse), qext_ref[...].astype(F32)
            ).astype(BF16)
            gx[half, :, :PAIR] = jnp.where(mine, grads, 0.0).astype(BF16)
            gx[half, :, PAIR:] = in_lanes(lane, split_three(-delta), 0.0).astype(BF16)
        dk_acc[...] = jnp.zeros_like(dk_acc)
        dv_acc[...] = jnp.zeros_like(dv_acc)

        def block(i, carry):
            rows = pl.ds(pl.multiple_of(i * QROWS, QROWS), QROWS)
            units = [(half, k) for k in range(0, length, KROWS) for half in range(2)]
            grad_queries = [None, None]

            def products_of(half, k):
                return (
                    dot_nt(kx[k : k + KROWS, :], qx[half, rows, :]),
                    dot_nt(vx[k : k + KROWS, :], gx[half, rows, :]),
                )

            ahead = products_of(*units[0])
            for n, (half, k) in enumerate(units):
                scores, grad_prob = ahead
                if n + 1 < len(units):
                    ahead = products_of(*units[n + 1])
                prob = jnp.exp(scores)
                grad_score = (prob * grad_prob).astype(BF16)
                dv_acc[k : k + KROWS, :] += dot(prob.astype(BF16), gx[half, rows, :PAIR])
                dk_acc[k : k + KROWS, :] += dot(grad_score, qx[half, rows, :PAIR])
                found = dot(kt[half * HEAD_DIM : (half + 1) * HEAD_DIM, k : k + KROWS], grad_score)
                grad_queries[half] = found if k == 0 else grad_queries[half] + found
            merged[rows, part] = (
                jnp.concatenate(grad_queries, axis=0).T * HEAD_DIM**-0.5
            ).astype(BF16)
            return carry

        lax.fori_loop(0, length // QROWS, block, 0)
        merged[:, GROUP + pair * PAIR : GROUP + (pair + 1) * PAIR] = dk_acc[...].astype(BF16)
        merged[:, 2 * GROUP + pair * PAIR : 2 * GROUP + (pair + 1) * PAIR] = dv_acc[
            ...
        ].astype(BF16)

    bias, found = [], []
    for j in range(3):
        grads = merged[:, j * GROUP : (j + 1) * GROUP]
        if j != 1:
            bias.append(jnp.sum(grads.astype(F32), axis=0, keepdims=True))
        dw = dot(xt_ref[...], grads).astype(BF16)
        if last:
            found.append(dw)
        else:
            dw_ref[j * width : (j + 1) * width, :] = dw
    bias = jnp.concatenate(bias + [jnp.zeros((6, GROUP), F32)], axis=0)
    if not last:
        gb_ref[...] = bias
        return
    half = send_ref.shape[0]
    bias = jnp.concatenate([ref[...] for ref in gb_refs] + [bias, jnp.zeros_like(bias)], axis=0)
    found = list(early_refs) + found + [bias.astype(BF16)]
    filler = 2 * half - sum(values.shape[0] for values in found)
    if filler:
        found.append(jnp.zeros((filler, GROUP), BF16))

    def put(refs):
        at = 0
        for values in found:
            done = 0
            while done < values.shape[0]:
                which, row = (at + done) // half, (at + done) % half
                count = min(values.shape[0] - done, half - row)
                refs[which][row : row + count, :] = values[done : done + count, :]
                done += count
            at += values.shape[0]

    @pl.when(bit_ref[0] == 0)
    def _():
        put((keep_ref, send_ref))

    @pl.when(bit_ref[0] != 0)
    def _():
        put((send_ref, keep_ref))


def backward_attention(group, bit, rows, biases, early, xt, kext, qext, lse, heads, deps):
    width, length = xt.shape
    last = bool(biases)
    operands = [xt, kext, qext, lse, *heads, *deps, *biases, *early]
    in_specs = [
        whole((width, length)),
        whole((length, PAIR)),
        whole((length, PAIR)),
        whole((length, PAIR)),
    ]
    in_specs += [columns_of(length, GROUP, group)] * 5
    in_specs += [pl.BlockSpec(memory_space=pl.ANY)] * len(deps)
    in_specs += [whole((8, GROUP))] * len(biases) + [whole((3 * width, GROUP))] * len(early)
    shape = jax.ShapeDtypeStruct
    if last:
        outs = [((rows // 2, GROUP), BF16)] * 2 + [((length, 3 * GROUP), BF16)]
    else:
        outs = [((3 * width, GROUP), BF16), ((length, 3 * GROUP), BF16), ((8, GROUP), F32)]

    def kernel(*refs):
        backward_attention_kernel(group, last, len(deps), *refs)

    return pl.pallas_call(
        kernel,
        grid=(1,),
        in_specs=[pl.BlockSpec(memory_space=pltpu.SMEM)] + in_specs,
        out_specs=[whole(o[0]) for o in outs] + [pl.BlockSpec(memory_space=pltpu.SMEM)],
        scratch_shapes=[
            pltpu.VMEM((2, length, 2 * PAIR), BF16),
            pltpu.VMEM((2, length, 2 * PAIR), BF16),
            pltpu.VMEM((length, 2 * PAIR), BF16),
            pltpu.VMEM((length, 2 * PAIR), BF16),
            pltpu.VMEM((PAIR, length), BF16),
            pltpu.VMEM((length, PAIR), F32),
            pltpu.VMEM((length, PAIR), F32),
        ],
        out_shape=[shape(*o) for o in outs] + [shape((1,), jnp.int32)],
        compiler_params=params(60),
        cost_estimate=cost(8 * 10**9, 10 * 10**6, 4 * length * length),
        name="attention_backward",
    )(bit, *operands)


def input_grad_kernel(resid_ref, m0_ref, m1_ref, m2_ref, w_ref, *refs):
    own_ref, other_ref, token = refs[-3:]
    token[0] = 0
    width = resid_ref.shape[1]
    total = resid_ref[...]
    for group, merged in enumerate((m0_ref, m1_ref, m2_ref)):
        columns = [
            w_ref[:, j * width + group * GROUP : j * width + (group + 1) * GROUP] for j in range(3)
        ]
        total = total + dot_nt(merged[...], jnp.concatenate(columns, axis=1))
    step = pl.program_id(0)

    @pl.when(step < pl.num_programs(0) // 2)
    def _():
        own_ref[...] = total

    @pl.when(step >= pl.num_programs(0) // 2)
    def _():
        other_ref[...] = total.astype(BF16)


def input_grad(resid, merged, w_qkv, deps):
    length, width = resid.shape
    half = length // TOKENS // 2
    shape = jax.ShapeDtypeStruct
    return pl.pallas_call(
        input_grad_kernel,
        grid=(2 * half,),
        in_specs=[rows_of(TOKENS, width)]
        + [rows_of(TOKENS, 3 * GROUP)] * len(merged)
        + [whole(w_qkv.shape)]
        + [pl.BlockSpec(memory_space=pl.ANY)] * len(deps),
        out_specs=[
            pl.BlockSpec((TOKENS, width), lambda i: (jnp.minimum(i, half - 1), 0)),
            pl.BlockSpec((TOKENS, width), lambda i: (jnp.maximum(i - half, 0), 0)),
            pl.BlockSpec(memory_space=pltpu.SMEM),
        ],
        out_shape=[
            shape((length // 2, width), F32),
            shape((length // 2, width), BF16),
            shape((1,), jnp.int32),
        ],
        compiler_params=params(60),
        cost_estimate=cost(4 * 10**9, 16 * 10**6),
        name="input_grad",
    )(resid, *merged, w_qkv, *deps)


def normalize(values):
    centered = values - jnp.mean(values, axis=1, keepdims=True)
    inverse = lax.rsqrt(jnp.mean(centered * centered, axis=1, keepdims=True) + EPSILON)
    return centered * inverse, inverse


def normalize_back(grads, hat, inverse):
    return inverse * (
        grads
        - jnp.mean(grads, axis=1, keepdims=True)
        - hat * jnp.mean(grads * hat, axis=1, keepdims=True)
    )


def gelu_and_slope(values):
    cumulative = 0.5 + 0.5 * lax.erf(values * 0.7071067811865476)
    bell = jnp.exp2(values * values * -0.7213475204444817)
    return values * cumulative, cumulative + values * bell * 0.3989422804014327


def forward_dense_kernel(
    ctx_ref, x_ref, og_ref, kext_ref, w_out_ref, w_inner_ref, w_final_ref,
    b_out_ref, g_one_ref, s_one_ref, b_inner_ref, b_final_ref, g_two_ref, s_two_ref,
    own_ref, other_ref, pooled_ref, low_ref, hat_ref, inv_ref, grad_ref, final_ref, slope_ref, dw_ref, gb_ref,
    act, final, sums, counts, pre,
):
    step = pl.program_id(0)
    count, width = x_ref.shape
    hidden = w_inner_ref.shape[1]
    rows = pl.ds(pl.multiple_of(step * count, count), count)

    @pl.when(step == 0)
    def _():
        sums[...] = jnp.zeros_like(sums)
        counts[...] = jnp.zeros_like(counts)
        gb_ref[...] = jnp.zeros_like(gb_ref)

    resid = x_ref[...].astype(F32) + dot(ctx_ref[...], w_out_ref[...]) + b_out_ref[...]
    hat, inverse = normalize(resid)
    hat_ref[...] = hat
    inv_ref[...] = jnp.broadcast_to(inverse, inv_ref.shape)
    normed = hat * g_one_ref[...] + s_one_ref[...]
    low = normed.astype(BF16)
    low_ref[...] = normed.T.astype(BF16)
    total = normed + b_final_ref[...]

    def inner_of(c):
        part = slice(c * CHUNK, (c + 1) * CHUNK)
        pre[c % 2] = dot(low, w_inner_ref[:, part])

    inner_of(0)
    for c in range(hidden // CHUNK):
        if c + 1 < hidden // CHUNK:
            inner_of(c + 1)
        for r in range(0, count, 32):
            for j in range(0, CHUNK, GROUP):
                part = slice(c * CHUNK + j, c * CHUNK + j + GROUP)
                inner = pre[c % 2, r : r + 32, j : j + GROUP] + b_inner_ref[:, part]
                gelu, slope = gelu_and_slope(inner)
                slope_ref[r : r + 32, part] = slope.astype(BF16)
                act[pl.ds(pl.multiple_of(step * count + r, 32), 32), part] = gelu.astype(BF16)
        part = slice(c * CHUNK, (c + 1) * CHUNK)
        total = total + dot(act[rows, part], w_final_ref[part, :])
    hat, inverse = normalize(total)
    layer_out = hat * g_two_ref[...] + s_two_ref[...]
    high = layer_out.astype(BF16)

    @pl.when(step < pl.num_programs(0) // 2)
    def _():
        own_ref[...] = high

    @pl.when(step >= pl.num_programs(0) // 2)
    def _():
        other_ref[...] = high

    rest = (layer_out - high.astype(F32)).astype(BF16)
    member = kext_ref[...]
    sums[...] += dot_tn(member, high) + dot_tn(member, rest)
    counts[...] += dot_tn(member, jnp.ones((count, PAIR), BF16))
    grads = og_ref[...].astype(F32)
    gb_ref[0:1, :] += jnp.sum(grads * hat, axis=0, keepdims=True)
    gb_ref[1:2, :] += jnp.sum(grads, axis=0, keepdims=True)
    grads = normalize_back(grads * g_two_ref[...], hat, inverse)
    grad_ref[...] = grads
    grads = grads.astype(BF16)
    final_ref[...] = grads
    final[:, rows] = grads.astype(F32).T.astype(BF16)
    gb_ref[2:3, :] += jnp.sum(grads.astype(F32), axis=0, keepdims=True)

    @pl.when(step == pl.num_programs(0) - 1)
    def _():
        pooled_ref[...] = sums[:NSEG, :] / jnp.maximum(counts[:NSEG, :1], 1.0)


        def chunk(c, carry):
            here = pl.ds(pl.multiple_of(c * width, width), width)
            dw_ref[here, :] = dot(final[...], act[:, here]).astype(BF16)
            return carry

        lax.fori_loop(0, hidden // width, chunk, 0)


def forward_dense(context, x, out_grad, kext, w_out, w_inner, w_final, vectors):
    length, width = x.shape
    hidden = w_inner.shape[1]
    half = length // TOKENS // 2
    shape = jax.ShapeDtypeStruct
    return pl.pallas_call(
        forward_dense_kernel,
        grid=(length // TOKENS,),
        in_specs=[rows_of(TOKENS, width)] * 3
        + [rows_of(TOKENS, PAIR), whole(w_out.shape), whole(w_inner.shape), whole(w_final.shape)]
        + [whole(v.shape) for v in vectors],
        out_specs=[
            pl.BlockSpec((TOKENS, width), lambda i: (jnp.minimum(i, half - 1), 0)),
            pl.BlockSpec((TOKENS, width), lambda i: (jnp.maximum(i - half, 0), 0)),
            whole((NSEG, width)),
            columns_of(width, TOKENS),
            rows_of(TOKENS, width),
            rows_of(TOKENS, PAIR),
            rows_of(TOKENS, width),
            rows_of(TOKENS, width),
            rows_of(TOKENS, hidden),
            whole((hidden, width)),
            whole((8, width)),
        ],
        out_shape=[
            shape((length // 2, width), BF16),
            shape((length // 2, width), BF16),
            shape((NSEG, width), F32),
            shape((width, length), BF16),
            shape((length, width), F32),
            shape((length, PAIR), F32),
            shape((length, width), F32),
            shape((length, width), BF16),
            shape((length, hidden), BF16),
            shape((hidden, width), BF16),
            shape((8, width), F32),
        ],
        scratch_shapes=[
            pltpu.VMEM((length, hidden), BF16),
            pltpu.VMEM((width, length), BF16),
            pltpu.VMEM((PAIR, width), F32),
            pltpu.VMEM((PAIR, PAIR), F32),
            pltpu.VMEM((2, TOKENS, CHUNK), F32),
        ],
        compiler_params=params(60),
        cost_estimate=cost(45 * 10**9, 45 * 10**6, length * hidden),
        name="dense_forward",
    )(context, x, out_grad, kext, w_out, w_inner, w_final, *vectors)


def backward_dense_kernel(deps, *refs):
    (
        final_ref, slope_ref, grad_ref, hat_ref, inv_ref,
        w_out_ref, w_inner_ref, w_final_ref, g_one_ref,
    ) = refs[:9]
    resid_ref, go_ref, inner_ref, attended_ref, gb_ref, gbi_ref, token = refs[9 + deps :]
    token[0] = 0
    step = pl.program_id(0)
    width = grad_ref.shape[1]
    hidden = w_inner_ref.shape[1]

    @pl.when(step == 0)
    def _():
        gb_ref[...] = jnp.zeros_like(gb_ref)
        gbi_ref[...] = jnp.zeros_like(gbi_ref)

    grads = grad_ref[...]
    for c in range(hidden // width):
        part = slice(c * width, (c + 1) * width)
        grad_act = dot_nt(final_ref[...], w_final_ref[part, :])
        grad_inner = (grad_act * slope_ref[:, part].astype(F32)).astype(BF16)
        inner_ref[:, part] = grad_inner
        gbi_ref[c : c + 1, :] += jnp.sum(grad_inner.astype(F32), axis=0, keepdims=True)
        grads = grads + dot_nt(grad_inner, w_inner_ref[:, part])
    hat = hat_ref[...]
    gb_ref[0:1, :] += jnp.sum(grads * hat, axis=0, keepdims=True)
    gb_ref[1:2, :] += jnp.sum(grads, axis=0, keepdims=True)
    grads = normalize_back(grads * g_one_ref[...], hat, inv_ref[:, :1])
    resid_ref[...] = grads
    low = grads.astype(BF16)
    gb_ref[2:3, :] += jnp.sum(low.astype(F32), axis=0, keepdims=True)
    attended_ref[...] = low
    go_ref[...] = dot_nt(low, w_out_ref[...]).astype(BF16)


def backward_dense(final, slope, grad_two, hat, inverse, w_out, w_inner, w_final, gain, deps):
    length, width = hat.shape
    hidden = w_inner.shape[1]
    shape = jax.ShapeDtypeStruct

    def kernel(*refs):
        backward_dense_kernel(len(deps), *refs)

    return pl.pallas_call(
        kernel,
        grid=(length // TOKENS,),
        in_specs=[
            rows_of(TOKENS, width),
            rows_of(TOKENS, hidden),
            rows_of(TOKENS, width),
            rows_of(TOKENS, width),
            rows_of(TOKENS, PAIR),
            whole(w_out.shape),
            whole(w_inner.shape),
            whole(w_final.shape),
            whole(gain.shape),
        ]
        + [pl.BlockSpec(memory_space=pl.ANY)] * len(deps),
        out_specs=[
            rows_of(TOKENS, width),
            rows_of(TOKENS, width),
            rows_of(TOKENS, hidden),
            rows_of(TOKENS, width),
            whole((8, width)),
            whole((8, width)),
            pl.BlockSpec(memory_space=pltpu.SMEM),
        ],
        out_shape=[
            shape((length, width), F32),
            shape((length, width), BF16),
            shape((length, hidden), BF16),
            shape((length, width), BF16),
            shape((8, width), F32),
            shape((8, width), F32),
            shape((1,), jnp.int32),
        ],
        compiler_params=params(60),
        cost_estimate=cost(8 * 10**9, 20 * 10**6),
        name="dense_backward",
    )(final, slope, grad_two, hat, inverse, w_out, w_inner, w_final, gain, *deps)


def dense_weights_kernel(deps, bit_ref, *refs):
    low_ref, inner_ref, ctx_ref, attended_ref, one_ref, bi_ref, two_ref = refs[:7]
    send_ref, keep_ref, token, dw_ref = refs[-4:]
    token[0] = 0
    step = pl.program_id(0)
    width = attended_ref.shape[1]
    last = pl.num_programs(0) - 1

    @pl.when(step < last)
    def _():
        here = pl.ds(pl.multiple_of(step * width, width), width)
        dw_ref[here, :] = dot(low_ref[...], inner_ref[...]).astype(BF16)

    @pl.when(step == last)
    def _():
        at = bi_ref.shape[0] // 2 * width
        dw_ref[at : at + width, :] = dot_tn(ctx_ref[...], attended_ref[...]).astype(BF16)
        at += width
        blocks = [one_ref[...], bi_ref[...], two_ref[...]]
        blocks.append(jnp.zeros((8, width), F32))
        dw_ref[at : at + 32, :] = jnp.concatenate(blocks, axis=0).astype(BF16)
        dw_ref[at + 32 :, :] = jnp.zeros_like(dw_ref[at + 32 :, :])
        half = send_ref.shape[0]
        send_ref[...] = dw_ref[pl.ds(pl.multiple_of((1 - bit_ref[0]) * half, half), half), :]
        keep_ref[...] = dw_ref[pl.ds(pl.multiple_of(bit_ref[0] * half, half), half), :]


def dense_weights(bit, rows, low, inner, context, attended, gb_one, gb_inner, gb_two, deps):
    width, length = low.shape
    hidden = inner.shape[1]
    blocks = hidden // width

    def kernel(*refs):
        dense_weights_kernel(len(deps), *refs)

    return pl.pallas_call(
        kernel,
        grid=(blocks + 1,),
        in_specs=[
            pl.BlockSpec(memory_space=pltpu.SMEM),
            whole((width, length)),
            pl.BlockSpec((length, width), lambda i: (0, jnp.minimum(i, blocks - 1))),
            whole((length, width)),
            whole((length, width)),
            whole((8, width)),
            whole((8, width)),
            whole((8, width)),
        ]
        + [pl.BlockSpec(memory_space=pl.ANY)] * len(deps),
        out_specs=[whole((rows // 2, width))] * 2 + [pl.BlockSpec(memory_space=pltpu.SMEM)],
        out_shape=[jax.ShapeDtypeStruct((rows // 2, width), BF16)] * 2
        + [jax.ShapeDtypeStruct((1,), jnp.int32)],
        scratch_shapes=[pltpu.VMEM((rows, width), BF16)],
        compiler_params=params(60),
        cost_estimate=cost(6 * 10**9, 16 * 10**6),
        name="dense_weights",
    )(bit, low, inner, context, attended, gb_one, gb_inner, gb_two, *deps)


def spread(own_ref, other_ref, scalars, rows, block, put):
    half = own_ref.shape[0]

    def move(ref, low, which):
        for piece in range(half // rows):
            start = which * half + piece * rows
            at = 0
            while at < rows:
                count = min(rows - at, block - (start + at) % block)
                here = pl.ds(pl.multiple_of((piece ^ low) * rows + at, math.gcd(rows, block)), count)
                put(start + at, ref[here, :].astype(F32))
                at += count

    for i, ref in enumerate((own_ref, other_ref)):
        for which in range(2):

            @pl.when(scalars[2 * i + 1] == which)
            def _():
                move(ref, scalars[2 * i], which)


def put_small(small_ref, row, values):
    count = min(values.shape[0], small_ref.shape[0] - row)
    if count > 0:
        small_ref[row : row + count, :] = values[:count, :]


def widen_dense_kernel(rows, piece_of, table_ref, final_ref, inner_ref, out_ref, small_ref, square):
    width, hidden = inner_ref.shape
    first, second = rows
    count = width // first
    for i in range(count):
        at = i * (first + second)
        square[i * first : (i + 1) * first, :] = table_ref[at : at + first, :]
        here = slice(at + first, at + first + second)
        start = piece_of[pl.program_id(0) * count + i] * second
        row = pl.ds(pl.multiple_of(start % width, second), second)

        @pl.when(start < hidden)
        def _():
            block = pl.ds(pl.multiple_of(start // width * width, width), width)
            inner_ref[row, block] = table_ref[here, :].astype(F32)

        @pl.when((start >= hidden) & (start < hidden + width))
        def _():
            out_ref[row, :] = table_ref[here, :].astype(F32)

        @pl.when(start == hidden + width)
        def _():
            small_ref[...] = table_ref[at + first : at + first + small_ref.shape[0], :].astype(F32)

    for r in range(0, width, UNIT):
        final_ref[r : r + UNIT, :] = square[:, r : r + UNIT].astype(F32).T


def widen_dense(owners, rows, table, hidden):
    width = table.shape[1]
    first, second = rows
    count = len(owners)
    if first * count == hidden and first % 16 == 0 and width % first == 0 and width % second == 0:
        piece_of = [0] * count
        for piece, device in enumerate(owners):
            piece_of[device] = piece
        shape = jax.ShapeDtypeStruct
        return pl.pallas_call(
            lambda *refs: widen_dense_kernel(rows, *refs),
            grid=(hidden // width,),
            in_specs=[
                pl.BlockSpec(memory_space=pltpu.SMEM),
                rows_of(width // first * (first + second), width),
            ],
            out_specs=[
                rows_of(width, width),
                whole((width, hidden)),
                whole((width, width)),
                whole((32, width)),
            ],
            out_shape=[
                shape((hidden, width), F32),
                shape((width, hidden), F32),
                shape((width, width), F32),
                shape((32, width), F32),
            ],
            scratch_shapes=[pltpu.VMEM((width, width), BF16)],
            compiler_params=params(48),
            cost_estimate=cost(0, 6 * table.size),
            name="widen_dense",
        )(jnp.array(piece_of, jnp.int32), table)
    pieces = table.reshape(count, first + second, width)
    squares = pieces[:, :first].reshape(hidden // width, width, width).astype(F32)
    other = jnp.concatenate([pieces[device, first:] for device in owners]).astype(F32)
    inner = other[:hidden].reshape(hidden // width, width, width)
    at = hidden + width
    return (
        squares.transpose(0, 2, 1).reshape(hidden, width),
        inner.transpose(1, 0, 2).reshape(width, hidden),
        other[hidden:at],
        other[at : at + 32],
    )


def widen_qkv_kernel(rows, scalars, own_ref, other_ref, out_ref, small_ref):
    width = out_ref.shape[0]

    def put(at, values):
        block, row = at // width, at % width
        if block < out_ref.shape[1] // GROUP:
            column = (block % 3) * width + (block // 3) * GROUP
            out_ref[row : row + values.shape[0], column : column + GROUP] = values
        else:
            put_small(small_ref, row + (block - out_ref.shape[1] // GROUP) * width, values)

    spread(own_ref, other_ref, scalars, rows, width, put)


def widen(kernel, rows, scalars, arrays, shapes, name):
    nbytes = sum(2 * a.size for a in arrays) + sum(4 * math.prod(s) for s in shapes)
    return pl.pallas_call(
        lambda *refs: kernel(rows, *refs),
        in_specs=[pl.BlockSpec(memory_space=pltpu.SMEM)]
        + [pl.BlockSpec(memory_space=pltpu.VMEM)] * len(arrays),
        out_specs=[pl.BlockSpec(memory_space=pltpu.VMEM)] * len(shapes),
        out_shape=[jax.ShapeDtypeStruct(s, F32) for s in shapes],
        compiler_params=pltpu.CompilerParams(vmem_limit_bytes=48 * 2**20),
        cost_estimate=cost(0, nbytes),
        name=name,
    )(scalars, *arrays)


def swap_rows(array, parts, after=0):
    if parts == 2:
        me = lax.axis_index("seq")
        own = lax.dynamic_index_in_dim(array, me, 0, keepdims=True)
        other = lax.dynamic_index_in_dim(array, 1 - me + after, 0, keepdims=True)
        got = lax.ppermute(other, "seq", [(0, 1), (1, 0)])
        return jnp.concatenate([own, got], axis=0)
    return lax.all_to_all(array, "seq", split_axis=0, concat_axis=0, tiled=True)


def swap_back(array, parts):
    return lax.all_to_all(array, "seq", split_axis=0, concat_axis=0, tiled=True)


class Slice:
    def __init__(self, n_dp, n_seq):
        dp_bits, seq_bits = n_dp.bit_length() - 1, n_seq.bit_length() - 1
        dp = [("dp", i) for i in range(dp_bits)]
        seq = [("seq", i) for i in range(seq_bits)]
        even = dp[:1] + dp[1:2] + seq
        odd = dp[:1] + seq[:1] + dp[1:2] + seq[1:]
        self.plans = (even, odd)
        self.halvings = len(even)
        self.ways = 1 << max(dp_bits - 2, 0)
        self.bits = dp_bits + seq_bits
        self.pairs = []
        for stage in range(self.halvings):
            pairs = []
            for d in range(n_dp):
                for s in range(n_seq):
                    axis, i = self.plans[d & 1][stage]
                    to = (d ^ (1 << i), s) if axis == "dp" else (d, s ^ (1 << i))
                    pairs.append((d * n_seq + s, to[0] * n_seq + to[1]))
            self.pairs.append(pairs)
        self.far_pairs = [
            [(d, d ^ (k << 2)) for d in range(n_dp)] for k in range(self.ways)
        ]
        self.index = {"dp": lax.axis_index("dp"), "seq": lax.axis_index("seq")}
        self.core = self.index["dp"] & 1
        self.place = self.index["dp"] >> 2
        self.mine = [self.bit(stage, self.core) for stage in range(self.halvings)]

    def bit(self, stage, core):
        even, odd = [(self.index[axis] >> i) & 1 for axis, i in (p[stage] for p in self.plans)]
        return jnp.where(core == 0, even, odd)

    def swap(self, array, stage):
        return lax.ppermute(array, ("dp", "seq"), self.pairs[stage])

    def far_swap(self, array, k):
        return lax.ppermute(array, "dp", self.far_pairs[k])

    def places(self):
        result = []
        for core, half in ((self.core, self.mine[0]), (self.core ^ 1, self.mine[0] ^ 1)):
            low = 0
            for stage in range(1, self.halvings):
                low = low * 2 + self.bit(stage, core)
            result += [low * self.ways + self.place, half]
        return jnp.stack([jnp.asarray(v, jnp.int32) for v in result])

    def owners(self, n_dp, n_seq):
        result = {}
        for d in range(n_dp):
            for s in range(n_seq):
                piece = 0
                for axis, i in self.plans[d & 1]:
                    piece = piece * 2 + (((d if axis == "dp" else s) >> i) & 1)
                result[piece * self.ways + (d >> 2)] = d * n_seq + s
        return [result[piece] for piece in range(n_dp * n_seq)]

    def padded(self, rows):
        unit = max(16 << self.bits, 2 * UNIT)
        return -(-rows // unit) * unit


def add_parts(rows, picks, keep, got, deps):
    count, width = keep.shape[0] // rows, keep.shape[1]

    def kernel(picks_ref, keep_ref, got_ref, *refs):
        refs[-1][0] = 0
        for i, out_ref in enumerate(refs[len(deps) : -1]):
            here = pl.ds(pl.multiple_of(picks_ref[i] * rows, rows), rows)
            out_ref[...] = (keep_ref[here, :].astype(F32) + got_ref[here, :].astype(F32)).astype(BF16)

    vmem = pl.BlockSpec(memory_space=pltpu.VMEM)
    smem = pl.BlockSpec(memory_space=pltpu.SMEM)
    return pl.pallas_call(
        kernel,
        in_specs=[smem, vmem, vmem] + [pl.BlockSpec(memory_space=pl.ANY)] * len(deps),
        out_specs=[vmem] * count + [smem],
        out_shape=[jax.ShapeDtypeStruct((rows, width), BF16)] * count
        + [jax.ShapeDtypeStruct((1,), jnp.int32)],
        compiler_params=pltpu.CompilerParams(vmem_limit_bytes=16 * 2**20),
        cost_estimate=cost(0, 6 * keep.size),
        name="add_parts",
    )(picks, keep, got, *deps)


class Table:
    def __init__(self, devices, send):
        self.devices = devices
        self.stage = 0
        self.keep = None
        self.sent = send
        self.got = devices.swap(send, 0)
        self.piece_rows = 2 * send.shape[0] >> devices.bits
        self.deps = [send]

    def advance(self, token=0, needs=()):
        devices = self.devices
        last = devices.halvings
        self.stage += 1
        stage = self.stage
        if stage < last:
            bit = devices.mine[stage] + token
            keep, got = (a.reshape(2, -1, a.shape[1]) for a in (self.keep, self.got))

            def added(i):
                parts = [
                    lax.dynamic_index_in_dim(a, i, 0, keepdims=False).astype(F32)
                    for a in (keep, got)
                ]
                return (parts[0] + parts[1]).astype(BF16)

            self.sent, self.keep = added(1 - bit), added(bit)
            self.got = devices.swap(self.sent, stage)
            self.deps = [self.sent, self.keep]
        elif stage == last:
            place = devices.place + token
            picks = jnp.stack([place ^ k for k in range(devices.ways)])
            rows = self.keep.shape[0] // devices.ways
            self.keep, *self.sent, self.token = add_parts(
                rows, picks, self.keep, self.got, list(needs)
            )
            self.got = [devices.far_swap(a, k + 1) for k, a in enumerate(self.sent)]
            self.deps = [self.keep, *self.sent]
        elif stage == last + 1:
            self.sent = self.total(token)
            self.got = [devices.far_swap(self.sent, k) for k in range(1, devices.ways)]
            self.deps = [self.sent]
        else:
            got = self.got if isinstance(self.got, list) else [self.got]
            if not isinstance(token, int):
                got = [jnp.where(token == 0, a, self.sent) for a in got]
            self.sent = jnp.concatenate([self.sent, *got], axis=0)
            self.got = devices.swap(self.sent, 2 * last + 1 - stage)
            self.deps = [self.sent]
        return self.deps

    def total(self, token):
        total = self.keep.astype(F32)
        for a in self.got:
            total = total + a.astype(F32)
        if not isinstance(token, int):
            total = jnp.where(token == 0, total, 0.0)
        return total.astype(BF16)

    def finish(self):
        while self.stage < 2 * self.devices.halvings + 1:
            self.advance()
        return self.sent, self.got


def on_device(
    tokens, segment_ids, w_qkv, b_qv, w_out, b_out, gain_one, shift_one,
    w_inner, b_inner, w_final, b_final, gain_two, shift_two, out_grad,
):
    parts, local_len, width = tokens.shape
    hidden = w_inner.shape[1]
    length = parts * local_len
    x = swap_rows(tokens, parts).reshape(length, width)
    segments = swap_rows(segment_ids, parts).reshape(length, 1)
    came = x[length - 1, width - 1]
    grads_in = swap_rows(out_grad, parts, (came != came).astype(jnp.int32)).reshape(length, width)

    slot = jnp.arange(PAIR, dtype=jnp.int32)[None, :]
    same = segments == slot
    kext = jnp.where(same | ((slot >= NSEG) & (slot < NSEG + 3)), 1.0, 0.0).astype(BF16)
    qext = jnp.where(same | (slot >= NSEG), 0.0, -FAR).astype(BF16)

    def row(vector):
        return vector.astype(F32).reshape(1, -1)

    devices = Slice(lax.axis_size("dp"), lax.axis_size("seq"))
    bit = jnp.asarray(devices.mine[0], jnp.int32).reshape(1)
    q, k, v, context, lse, xt = forward_attention(
        x, kext, qext, w_qkv, row(b_qv[0]), row(b_qv[1])
    )
    vectors = [
        row(v_) for v_ in (b_out, gain_one, shift_one, b_inner, b_final, gain_two, shift_two)
    ]
    (
        own_out, other_out, pooled, low, hat, inverse, grad_two, grad_final, slope, dw_final,
        gb_two,
    ) = forward_dense(
        context, x, grads_in, kext, w_out, w_inner, w_final, vectors
    )
    sum_final = lax.psum_scatter(dw_final, ("dp", "seq"), scatter_dimension=0, tiled=True)
    if parts == 2:
        me = lax.axis_index("seq")
        got = lax.ppermute(other_out, "seq", [(0, 1), (1, 0)])
        output_block = jnp.where(me == 0, jnp.stack([own_out, got]), jnp.stack([got, own_out]))
        other = lax.ppermute(pooled, "seq", [(0, 1), (1, 0)])
        pooled_all = jnp.where(me == 0, jnp.stack([pooled, other]), jnp.stack([other, pooled]))
    else:
        output = jnp.concatenate([own_out, other_out], axis=0)
        output_block = swap_back(output.reshape(parts, local_len, width), parts)
        pooled_all = lax.all_gather(pooled, "seq", axis=0)
    resid_grad, grad_context, grad_inner, attended, gb_one, gb_inner, token = backward_dense(
        grad_final, slope, grad_two, hat, inverse, w_out, w_inner, w_final, row(gain_one),
        [],
    )
    send, keep, token = dense_weights(
        bit, devices.padded(hidden + width + 32), low, grad_inner, context, attended,
        gb_one, gb_inner, gb_two, [output_block, pooled_all],
    )
    t_inner = Table(devices, send)
    t_inner.keep = keep
    heads = (q, k, v, grad_context, context)
    groups = width // GROUP
    qkv_rows = devices.padded(3 * width * groups + 8 * groups + 8)
    early, merged, biases = [], [], []
    for group in range(groups):
        last = group == groups - 1
        deps = t_inner.advance(token[0]) if group else t_inner.deps
        *found, token = backward_attention(
            group, bit, qkv_rows, biases if last else [], early if last else [],
            xt, kext, qext, lse, heads, deps,
        )
        merged.append(found[-1] if last else found[1])
        if not last:
            early.append(found[0])
            biases.append(found[2])
    t_qkv = Table(devices, found[0])
    t_qkv.keep = found[1]
    own_x, other_x, token = input_grad(resid_grad, merged, w_qkv, [])
    if parts == 2:
        got = lax.ppermute(other_x, "seq", [(0, 1), (1, 0)]).astype(F32)
        input_block = jnp.where(me == 0, jnp.stack([own_x, got]), jnp.stack([got, own_x]))
    else:
        grad_x = jnp.concatenate([own_x.astype(BF16), other_x], axis=0)
        input_block = swap_back(grad_x.reshape(parts, local_len, width), parts).astype(F32)
    t_qkv.advance(token[0])
    while t_inner.stage < devices.halvings:
        t_inner.advance(token[0], t_qkv.deps)
    while t_qkv.stage < devices.halvings:
        t_qkv.advance(t_inner.token[0], [input_block])
    pieces = (sum_final.shape[0], t_inner.piece_rows)
    all_dense = lax.all_gather(
        jnp.concatenate([sum_final, t_inner.total(0)]), ("dp", "seq"), axis=0, tiled=True
    )
    places = devices.places()
    wide_qkv, small_qv = widen(
        widen_qkv_kernel, t_qkv.piece_rows, places, t_qkv.finish(),
        [(width, 3 * width), (8 * groups + 8, GROUP)], "widen_qkv",
    )
    owners = devices.owners(lax.axis_size("dp"), lax.axis_size("seq"))
    wide_final, wide_inner, wide_out, small = widen_dense(owners, pieces, all_dense, hidden)

    gb_qv = jnp.stack(
        [jnp.concatenate([small_qv[8 * g + j] for g in range(groups)]) for j in range(2)]
    )
    return (
        output_block,
        pooled_all,
        input_block,
        wide_qkv,
        gb_qv,
        wide_out,
        small[2],
        small[0],
        small[1],
        wide_inner,
        small[8 : 8 + hidden // width].reshape(-1),
        wide_final,
        small[18],
        small[16],
        small[17],
    )


def solution(mesh):
    rows = P("dp", "seq", None)
    return jax.shard_map(
        on_device,
        mesh=mesh,
        in_specs=(rows, P("dp", "seq")) + (P(),) * 12 + (rows,),
        out_specs=(rows, P("dp", None, None), rows) + (P(),) * 12,
        check_vma=False,
    )
```
